128 devices in a mesh: slab: 8 (over y, core), pencil: 16 (over x, z).
Axes of the slice: x: 4, y: 4, z: 4, core: 2. Of those that a mesh axis runs over, the one named last changes fastest.
Arguments:
- features: bfloat16 [64, 1048576], P(None, ('slab', 'pencil')), may hold values from -6 to 6
- cotangent: bfloat16 [64, 1048576], P(None, ('slab', 'pencil')), may hold values from -6 to 6
- positions: int32 [3, 1048576], P(None, ('slab', 'pencil')), may hold values from 0 to 65535
- tiles: int32 [128], P(('slab', 'pencil')), may hold values from 1 to 64, 4096 in all
- weight: float32 [2048, 2, 4096], P(('slab', 'pencil')), may hold values from -6 to 6
Outputs:
- grad_features: float32 [64, 1048576], P(None, ('slab', 'pencil'))
- grad_weight: float32 [2048, 2, 4096], P(('slab', 'pencil'))
The draws below stay inside these ranges and needn't reach their ends.
Inputs may be any that keep to these rules, and one draw needn't show every extreme that they name: tiles[b] counts the live 128-row tiles at the start of brick b; the rest of the brick is padding. The counts sum to 4096, and some brick is full.
All inputs are finite; a program needn't handle non-finite values. No bound on the sum of `tiles` on one device may be relied on, other than what follows from the above.
Results may differ from the reference program's by a relative error of at most 0.0052.
Values may be sent and summed in bfloat16 or wider, within the bound.
A program may use at most 64 MiB of HBM per device.

```python
import math
import jax
import jax.numpy as jnp
import numpy as np
from jax import lax

C = 64
GRID = 256
KX = 16
KY = 16
KZ = 8
TILE = 128
TILES_DEV = 32
CAP_TILES = 64
CAP_ROWS = 8192
BRICKS = 128
ROWS = 1048576
LIVE = 524288
KM = 2048


fraction_steps = 256


def draw_positions(key, part):
    key = jax.random.fold_in(key, 11)
    key_cells, key_fraction = jax.random.split(key, 2)
    row_ids = jnp.arange(ROWS, dtype=jnp.int32)
    cell_table = jax.random.randint(key_cells, (3, ROWS), 0, GRID, dtype=jnp.int32)
    fractions = jax.random.randint(key_fraction, (3, ROWS), 0, fraction_steps, dtype=jnp.int32)
    coords = cell_table * fraction_steps + fractions
    coords = jnp.where(row_ids[None, :] == 1, 0, coords)
    coords = jnp.where(row_ids[None, :] == (BRICKS - 1) * CAP_ROWS, GRID * fraction_steps - 1, coords)
    return coords.astype(jnp.int32)


def steps_of(own_key, dims, cuts, low, top_value):
    def one(dim, shards_of):
        steps = jax.random.uniform(jax.random.fold_in(jax.random.fold_in(own_key, 6), dim), (shards_of,), jnp.float32, low / len(cuts), top_value / len(cuts))
        return jnp.repeat(jnp.exp(steps), dims[dim] // shards_of).reshape((-1,) + (1,) * (len(dims) - dim - 1))

    factor_of = one(*cuts[0])
    for cut in cuts[1:]:
        factor_of = factor_of * one(*cut)
    return factor_of


def length_profile(number_of, total, bound, slope):
    portions = [(1 << 20) // math.isqrt(grade ** slope) + 1 for grade in range(2, number_of + 1)]
    spare, given = total - bound - (number_of - 1), [1] * (number_of - 1)
    while spare > 0:
        free = [i for i in range(number_of - 1) if given[i] < bound]
        mass, budget = sum([portions[i] for i in free]), spare
        for i in free:
            addition = min(bound - given[i], max(1, budget * portions[i] // mass), spare)
            given[i] = given[i] + addition
            spare = spare - addition
    return np.array([bound] + given)


def ragged_sizes(key, count, total, bound, lean):
    if count == 2:
        one = jax.random.randint(key, (), max(1, total - bound), min(bound, total - 1) + 1)
        return jnp.stack([one, total - one])
    tallies = jnp.asarray(length_profile(count, total, bound, lean), jnp.int32)
    couples = (count - 1) // 2
    source_of, receiver = tallies[1:1 + 2 * couples:2], tallies[2:2 + 2 * couples:2]
    margin = jnp.minimum(source_of - 1, bound - receiver)
    shifted = jax.random.randint(jax.random.fold_in(key, 1), (couples,), 0, 1 << 20) % (margin + 1)
    tallies = tallies.at[1:1 + 2 * couples:2].set(source_of - shifted).at[2:2 + 2 * couples:2].set(receiver + shifted)
    return tallies[jax.random.permutation(jax.random.fold_in(key, 2), count)]


def bell_draw(rng, extent, width, reach, cuts=(), kind=jnp.bfloat16):
    factor_of = steps_of(rng, extent, cuts, -0.22, 0.18) if cuts else 1.0
    drawn = jax.random.normal(rng, extent, jnp.float32) * width * factor_of
    return jnp.minimum(jnp.maximum(drawn, -reach), reach).astype(kind)


def setup_inputs(seed: int = 0) -> dict:
    arg_keys = jax.random.split(jax.random.key(seed), 6)
    features = bell_draw(arg_keys[0], (C, ROWS), 1.0, 6.0, ((1, 128),))
    cotangent = bell_draw(arg_keys[1], (C, ROWS), 1.0, 6.0, ((1, 128),))
    positions = draw_positions(jax.random.fold_in(arg_keys[5], 71), 0)
    tiles = ragged_sizes(arg_keys[3], BRICKS, TILES_DEV * BRICKS, CAP_TILES, 2).astype(jnp.int32)
    weight = bell_draw(arg_keys[4], (KM, 2, C * C), 1.0, 6.0, ((0, 128),), jnp.float32)
    return {"features": features, "cotangent": cotangent, "positions": positions, "tiles": tiles, "weight": weight}


fraction_steps = 256
highest = lax.Precision.HIGHEST
contract_last = (((1,), (1,)), ((), ()))

def spline_weights(fraction):
    complement = 1.0 - fraction
    square = fraction * fraction
    cubed = square * fraction
    return jnp.stack([complement * complement * complement / 6.0, (3.0 * cubed - 6.0 * square + 4.0) / 6.0, (-3.0 * cubed + 3.0 * square + 3.0 * fraction + 1.0) / 6.0, cubed / 6.0])

def axis_phase(position, wave_numbers):
    cell_index = position // fraction_steps
    fraction = (position % fraction_steps).astype(jnp.float32) / fraction_steps
    weights = spline_weights(fraction)
    shifts = jnp.arange(4, dtype=jnp.int32) - 1
    stencil_cells = cell_index[None, :] + shifts[:, None]
    phase_turns = jnp.mod(wave_numbers[:, None, None] * stencil_cells[None, :, :], GRID)
    angles = phase_turns.astype(jnp.float32) * (2.0 * math.pi / GRID)
    real_part = lax.optimization_barrier(jnp.sum(weights[None] * jnp.cos(angles), axis=1))
    imag_part = -lax.optimization_barrier(jnp.sum(weights[None] * jnp.sin(angles), axis=1))
    return (real_part, imag_part)

def tile_phases(position):
    lead_waves = jnp.arange(KX, dtype=jnp.int32) - KX // 2
    side_waves = jnp.arange(KY, dtype=jnp.int32) - KY // 2
    depth_waves = jnp.arange(KZ, dtype=jnp.int32)
    lead_real, lead_imag = axis_phase(position[0], lead_waves)
    side_real, side_imag = axis_phase(position[1], side_waves)
    depth_real, depth_imag = axis_phase(position[2], depth_waves)
    columns = position.shape[1]
    pair_real = (side_real[:, None, :] * depth_real[None] - side_imag[:, None, :] * depth_imag[None]).reshape(KY * KZ, columns)
    pair_imag = (side_real[:, None, :] * depth_imag[None] + side_imag[:, None, :] * depth_real[None]).reshape(KY * KZ, columns)
    return (lead_real, lead_imag, pair_real.astype(jnp.bfloat16), pair_imag.astype(jnp.bfloat16))

def product_last(matrix, second):
    return lax.dot_general(matrix, second, contract_last, preferred_element_type=jnp.float32)

def spread_tile(values, phases):
    lead_real, lead_imag, pair_real, pair_imag = phases
    columns = values.shape[1]
    rows_real = (values[:, None, :] * lead_real[None]).reshape(-1, columns).astype(jnp.bfloat16)
    rows_imag = (values[:, None, :] * lead_imag[None]).reshape(-1, columns).astype(jnp.bfloat16)
    return (product_last(rows_real, pair_real) - product_last(rows_imag, pair_imag), product_last(rows_real, pair_imag) + product_last(rows_imag, pair_real))

def sample_tile(spectrum_real, spectrum_imag, phases):
    lead_real, lead_imag, pair_real, pair_imag = phases
    columns = pair_real.shape[1]
    mixed_real = jnp.dot(spectrum_real, pair_real, preferred_element_type=jnp.float32) + jnp.dot(spectrum_imag, pair_imag, preferred_element_type=jnp.float32)
    mixed_imag = jnp.dot(spectrum_real, pair_imag, preferred_element_type=jnp.float32) - jnp.dot(spectrum_imag, pair_real, preferred_element_type=jnp.float32)
    mixed_real = mixed_real.reshape(-1, KX, columns)
    mixed_imag = mixed_imag.reshape(-1, KX, columns)
    return lax.optimization_barrier(jnp.sum(mixed_real * lead_real[None] - mixed_imag * lead_imag[None], axis=1))

def mode_work(shared, weight):
    channels = C
    modes_here = weight.shape[0]
    filters = weight.reshape(modes_here, 2, channels, channels)
    feat_real, feat_imag = (shared[0, :channels], shared[1, :channels])
    cot_real, cot_imag = (shared[0, channels:], shared[1, channels:])

    def mixing(matrix, vector):
        return jnp.einsum('kco,ok->ck', matrix, vector, precision=highest)
    grad_real = mixing(filters[:, 0], cot_real) + mixing(filters[:, 1], cot_imag)
    grad_imag = mixing(filters[:, 0], cot_imag) - mixing(filters[:, 1], cot_real)
    feat_real_t, feat_imag_t = (feat_real.T[:, :, None], feat_imag.T[:, :, None])
    cot_real_t, cot_imag_t = (cot_real.T[:, None, :], cot_imag.T[:, None, :])
    weight_real = feat_real_t * cot_real_t + feat_imag_t * cot_imag_t
    weight_imag = feat_real_t * cot_imag_t - feat_imag_t * cot_real_t
    grad_weight = jnp.stack([weight_real, weight_imag], axis=1).reshape(modes_here, 2, channels * channels)
    return (grad_real, grad_imag, grad_weight)

def reference(features, cotangent, positions, tiles, weight):
    scale = 1.0 / math.sqrt(LIVE)
    stacked = jnp.concatenate([features, cotangent], axis=0)
    tile_total = ROWS // TILE

    def tile_live(tile_index):
        return tile_index % CAP_TILES < tiles[tile_index // CAP_TILES]

    def spread_step(tile_index, running):
        start_col = (tile_index * TILE).astype(jnp.int32)

        def add_tile(current):
            tile_block = lax.dynamic_slice_in_dim(stacked, start_col, TILE, 1).astype(jnp.float32)
            tile_place = lax.dynamic_slice_in_dim(positions, start_col, TILE, 1)
            part_real, part_imag = spread_tile(tile_block, tile_phases(tile_place))
            return (current[0] + part_real, current[1] + part_imag)

        def keep_sums(current):
            return current
        return lax.cond(tile_live(tile_index), add_tile, keep_sums, running)
    zero_sums = jnp.zeros((2 * C * KX, KY * KZ), jnp.float32)
    sum_real, sum_imag = lax.fori_loop(0, tile_total, spread_step, (zero_sums, zero_sums))
    shared = jnp.stack([sum_real, sum_imag]).reshape(2, 2 * C, KM) * scale
    grad_real, grad_imag, grad_weight = mode_work(shared, weight)
    spec_real = grad_real.reshape(C * KX, KY * KZ).astype(jnp.bfloat16)
    spec_imag = grad_imag.reshape(C * KX, KY * KZ).astype(jnp.bfloat16)

    def sample_step(tile_index, result):
        start_col = (tile_index * TILE).astype(jnp.int32)

        def write_tile(current):
            tile_place = lax.dynamic_slice_in_dim(positions, start_col, TILE, 1)
            values = sample_tile(spec_real, spec_imag, tile_phases(tile_place)) * scale
            return lax.dynamic_update_slice_in_dim(current, values, start_col, 1)

        def keep_result(current):
            return current
        return lax.cond(tile_live(tile_index), write_tile, keep_result, result)
    gradient = lax.fori_loop(0, tile_total, sample_step, jnp.zeros((C, ROWS), jnp.float32))
    return (gradient, grad_weight)
```

```python
import functools
import math

import jax
import jax.numpy as jnp
import numpy as np
from jax import lax
from jax.experimental import pallas as pl
from jax.experimental.pallas import tpu as pltpu
from jax.sharding import PartitionSpec as P

GRID = 256
KX = 16
KY = 16
KZ = 8
TILE = 128
TILES_DEV = 32
CHANNELS = 64
PAIRS = KY * KZ
HALF = KX // 2
ROWS_L = 2 * HALF + 1
ROWS_L_PAD = 24
STEP_FRACTION = 256
SLABS = 8
PENCILS = 16
MODES = 16

bf16 = jnp.bfloat16
f32 = jnp.float32
last_last = (((1,), (1,)), ((), ()))
MESH_ID = pl.DeviceIdType.MESH
VMEM_LIMIT = 56 * 1024 * 1024


def spline_table(waves):
    basis = np.array(
        [[1, -3, 3, -1], [4, 0, -6, 3], [1, 3, 3, -3], [0, 0, 0, 1]], np.float64
    ) / 6.0
    turn = np.exp(-2j * np.pi * np.outer(waves, np.arange(4) - 1) / GRID)
    return turn @ basis


def column(values):
    rows = lax.broadcasted_iota(jnp.int32, (8, 1), 0)
    out = jnp.full((8, 1), float(values[0]), f32)
    for row in range(1, 8):
        out = jnp.where(rows == row, float(values[row]), out)
    return out


def axis_phase(position, first_wave):
    columns = position.shape[1]
    table = spline_table(np.arange(first_wave, first_wave + 8))
    wave = lax.broadcasted_iota(jnp.int32, (8, 1), 0) + first_wave
    cell = position // STEP_FRACTION
    fraction = (position % STEP_FRACTION).astype(f32) * (1.0 / STEP_FRACTION)
    turns = (wave * cell + GRID // 2) % GRID - GRID // 2
    half = turns.astype(f32) * (math.pi / GRID)
    square = half * half
    sine = -1.0 / 39916800.0
    for term in (1.0 / 362880.0, -1.0 / 5040.0, 1.0 / 120.0, -1.0 / 6.0, 1.0):
        sine = sine * square + term
    sine = sine * half
    cosine = 1.0 / 479001600.0
    for term in (-1.0 / 3628800.0, 1.0 / 40320.0, -1.0 / 720.0, 1.0 / 24.0, -0.5, 1.0):
        cosine = cosine * square + term
    turn_cos = 1.0 - 2.0 * sine * sine
    turn_sin = 2.0 * sine * cosine
    fraction = jnp.broadcast_to(fraction, (8, columns))
    stencil_real = column(table[:, 3].real)
    stencil_imag = column(table[:, 3].imag)
    for power in (2, 1, 0):
        stencil_real = stencil_real * fraction + column(table[:, power].real)
        stencil_imag = stencil_imag * fraction + column(table[:, power].imag)
    real = turn_cos * stencil_real + turn_sin * stencil_imag
    imag = turn_cos * stencil_imag - turn_sin * stencil_real
    return real, imag


def write_phases(position, live, lead_ref, pair_ref, where):
    lead_real, lead_imag = axis_phase(position[0:1], 1)
    side_real, side_imag = axis_phase(position[1:2], 1)
    depth_real, depth_imag = axis_phase(position[2:3], 0)
    lead_ref[0:8, where] = lead_real * live
    lead_ref[8:16, where] = lead_imag * live
    lead_ref[16:24, where] = jnp.broadcast_to(live, lead_real.shape)
    reals, imags = [None] * KY, [None] * KY
    reals[HALF], imags[HALF] = depth_real, depth_imag
    for wave in range(1, HALF + 1):
        real, imag = side_real[wave - 1 : wave], side_imag[wave - 1 : wave]
        rr, ii = real * depth_real, imag * depth_imag
        ri, ir = real * depth_imag, imag * depth_real
        if wave < HALF:
            reals[HALF + wave], imags[HALF + wave] = rr - ii, ri + ir
        reals[HALF - wave], imags[HALF - wave] = rr + ii, ri - ir
    for pair in range(HALF):
        rows = pl.ds(pair * 16, 16)
        pair_ref[rows, where] = jnp.concatenate(reals[2 * pair : 2 * pair + 2], 0).astype(bf16)
        rows = pl.ds(PAIRS + pair * 16, 16)
        pair_ref[rows, where] = jnp.concatenate(imags[2 * pair : 2 * pair + 2], 0).astype(bf16)


def identity_matrix():
    rows = lax.broadcasted_iota(jnp.int32, (128, 128), 0)
    columns = lax.broadcasted_iota(jnp.int32, (128, 128), 1)
    return jnp.where(rows == columns, 1.0, 0.0).astype(bf16)


def flipped(matrix, eye):
    return lax.dot_general(eye, matrix, last_last, preferred_element_type=f32)


def spread_kernel(chunk, tiles_ref, feat_ref, cot_ref, pos_ref, part_ref, pair_ref, lead_ref, rows, acc):
    step = pl.program_id(0)

    @pl.when(step == 0)
    def _():
        acc[...] = jnp.zeros_like(acc)

    sub = 512
    for piece in range(chunk // sub):
        where = slice(piece * sub, (piece + 1) * sub)
        index = step * chunk + piece * sub + lax.broadcasted_iota(jnp.int32, (1, sub), 1)
        live = jnp.where(index < tiles_ref[0] * TILE, 1.0, 0.0).astype(f32)
        write_phases(pos_ref[:, where], live, lead_ref, pair_ref, where)
    feat = feat_ref[...].astype(f32)
    cot = cot_ref[...].astype(f32)
    for row in range(ROWS_L):
        factor = lead_ref[row : row + 1, :]
        rows[row * 128 : row * 128 + 64, :] = (feat * factor).astype(bf16)
        rows[row * 128 + 64 : row * 128 + 128, :] = (cot * factor).astype(bf16)
    acc[...] += lax.dot_general(rows[...], pair_ref[...], last_last, preferred_element_type=f32)

    @pl.when(step == pl.num_programs(0) - 1)
    def _():
        eye = identity_matrix()

        def put(index, real, imag):
            both = flipped(jnp.concatenate([real, imag], 0).astype(bf16), eye).astype(bf16)
            part_ref[index, 0] = both[:, 0:128]
            part_ref[index, 1] = both[:, 128:256]

        def sums(row):
            return acc[row * 128 : (row + 1) * 128, 0:PAIRS], acc[row * 128 : (row + 1) * 128, PAIRS:]

        put(HALF, *sums(2 * HALF))
        for wave in range(1, HALF + 1):
            rr, ri = sums(wave - 1)
            ir, ii = sums(HALF + wave - 1)
            if wave < HALF:
                put(HALF + wave, rr - ii, ri + ir)
            put(HALF - wave, rr + ii, ri - ir)


def spread_call(features, cotangent, positions, tiles):
    atoms = features.shape[1]
    chunk = 1024
    return pl.pallas_call(
        functools.partial(spread_kernel, chunk),
        grid=(atoms // chunk,),
        out_shape=[
            jax.ShapeDtypeStruct((KX, 2, PAIRS, 2 * CHANNELS), bf16),
            jax.ShapeDtypeStruct((2 * PAIRS, atoms), bf16),
            jax.ShapeDtypeStruct((ROWS_L_PAD, atoms), f32),
        ],
        in_specs=[
            pl.BlockSpec(memory_space=pltpu.SMEM),
            pl.BlockSpec((CHANNELS, chunk), lambda i: (0, i)),
            pl.BlockSpec((CHANNELS, chunk), lambda i: (0, i)),
            pl.BlockSpec((3, chunk), lambda i: (0, i)),
        ],
        out_specs=[
            pl.BlockSpec((KX, 2, PAIRS, 2 * CHANNELS), lambda i: (0, 0, 0, 0)),
            pl.BlockSpec((2 * PAIRS, chunk), lambda i: (0, i)),
            pl.BlockSpec((ROWS_L_PAD, chunk), lambda i: (0, i)),
        ],
        scratch_shapes=[
            pltpu.VMEM((ROWS_L * 128, chunk), bf16),
            pltpu.VMEM((ROWS_L * 128, 2 * PAIRS), f32),
        ],
        compiler_params=pltpu.CompilerParams(vmem_limit_bytes=VMEM_LIMIT),
        name="spread",
    )(tiles, features, cotangent, positions)


def split_product(values, matrix):
    high = values.astype(bf16)
    low = (values - high.astype(f32)).astype(bf16)
    return jnp.dot(high, matrix, preferred_element_type=f32) + jnp.dot(
        low, matrix, preferred_element_type=f32
    )


def both_halves(values, upper):
    part = values[:, 64:128] if upper else values[:, 0:64]
    return jnp.concatenate([part, part], 1)


def exchange_kernel(
    scale,
    part_ref,
    weight_ref,
    spectrum_ref,
    grad_ref,
    from_slab,
    slab_sum,
    from_pencil,
    products,
    own_block,
    send_slab,
    recv_slab,
    send_pencil,
    recv_pencil,
    send_grad,
    recv_grad,
    send_full,
    recv_full,
):
    slab = lax.axis_index("slab")
    pencil = lax.axis_index("pencil")
    barrier = pltpu.get_barrier_semaphore()

    def slab_peer(step):
        return lax.rem(slab + step, SLABS)

    def pencil_peer(step):
        return lax.rem(pencil + step, PENCILS)

    def greet_slab(step, _):
        pl.semaphore_signal(barrier, inc=1, device_id=(slab_peer(step), pencil), device_id_type=MESH_ID)
        return 0

    def greet_pencil(step, _):
        pl.semaphore_signal(barrier, inc=1, device_id=(slab, pencil_peer(step)), device_id_type=MESH_ID)
        return 0

    lax.fori_loop(1, SLABS, greet_slab, 0)
    lax.fori_loop(1, PENCILS, greet_pencil, 0)
    pl.semaphore_wait(barrier, SLABS - 1 + PENCILS - 1)

    def send_to_slab(step, _):
        peer = slab_peer(step)
        pltpu.make_async_remote_copy(
            src_ref=part_ref.at[pl.ds(peer * 2, 2)],
            dst_ref=from_slab.at[SLABS - 1 - step],
            send_sem=send_slab,
            recv_sem=recv_slab,
            device_id=(peer, pencil),
            device_id_type=MESH_ID,
        ).start()
        return 0

    lax.fori_loop(1, SLABS, send_to_slab, 0)
    pltpu.make_async_copy(from_slab, from_slab, recv_slab).wait()
    for parity in range(2):
        for side in range(2):
            total = part_ref[slab * 2 + parity, side].astype(f32)
            for source in range(SLABS - 1):
                total = total + from_slab[source, parity, side].astype(f32)
            slab_sum[parity, side] = total

    def send_to_pencil(step, _):
        peer = pencil_peer(step)
        pltpu.make_async_remote_copy(
            src_ref=slab_sum.at[peer // 8, :, pl.ds(pl.multiple_of(peer % 8 * MODES, MODES), MODES), :],
            dst_ref=from_pencil.at[PENCILS - 1 - step],
            send_sem=send_pencil,
            recv_sem=recv_pencil,
            device_id=(slab, peer),
            device_id_type=MESH_ID,
        ).start()
        return 0

    lax.fori_loop(1, PENCILS, send_to_pencil, 0)
    own_rows = pl.ds(pl.multiple_of(pencil % 8 * MODES, MODES), MODES)
    pltpu.make_async_copy(from_pencil, from_pencil, recv_pencil).wait()
    sides = []
    for side in range(2):
        total = slab_sum[pencil // 8, side, own_rows, :]
        for source in range(PENCILS - 1):
            total = total + from_pencil[source, side]
        total = total * scale
        spectrum_ref[side] = total
        sides.append(both_halves(total, True))
    g_real, g_imag = sides
    lanes = lax.broadcasted_iota(jnp.int32, (MODES, 128), 1)
    halves = jnp.where(
        lax.broadcasted_iota(jnp.int32, (128, 128), 0) // 64
        == lax.broadcasted_iota(jnp.int32, (128, 128), 1) % 2,
        1.0,
        0.0,
    ).astype(bf16)
    for tile in range(CHANNELS // 2):
        w_real = weight_ref[:, 0, tile * 128 : (tile + 1) * 128]
        w_imag = weight_ref[:, 1, tile * 128 : (tile + 1) * 128]
        products[0, tile * MODES : (tile + 1) * MODES] = w_real * g_real + w_imag * g_imag
        products[1, tile * MODES : (tile + 1) * MODES] = w_real * g_imag - w_imag * g_real
    real_sums = split_product(products[0], halves)
    imag_sums = split_product(products[1], halves)
    block = jnp.zeros((MODES, 128), f32)
    for tile in range(CHANNELS // 2):
        rows = slice(tile * MODES, (tile + 1) * MODES)
        mixed = jnp.where(lanes < 64, real_sums[rows], imag_sums[rows])
        block = block + jnp.where(lanes % 64 // 2 == tile, mixed, 0.0)
    own_block[...] = block.astype(bf16)
    here = slab * 2 + pencil // 8

    grad_ref[here, own_rows, :] = own_block[...]

    def share_block(step, _):
        peer = pencil_peer(step)
        pltpu.make_async_remote_copy(
            src_ref=own_block,
            dst_ref=grad_ref.at[here, own_rows, :],
            send_sem=send_grad,
            recv_sem=recv_grad,
            device_id=(slab, peer),
            device_id_type=MESH_ID,
        ).start()
        return 0

    lax.fori_loop(1, PENCILS, share_block, 0)
    pltpu.make_async_copy(
        from_pencil.at[pl.ds(0, PENCILS - 1), 0, pl.ds(0, 8), :],
        from_pencil.at[pl.ds(0, PENCILS - 1), 0, pl.ds(0, 8), :],
        recv_grad,
    ).wait()
    mine = pl.ds(slab * 2, 2)

    def share_slab(step, _):
        peer = slab_peer(step)
        pltpu.make_async_remote_copy(
            src_ref=grad_ref.at[mine],
            dst_ref=grad_ref.at[mine],
            send_sem=send_full,
            recv_sem=recv_full,
            device_id=(peer, pencil),
            device_id_type=MESH_ID,
        ).start()
        return 0

    lax.fori_loop(1, SLABS, share_slab, 0)
    pltpu.make_async_copy(
        grad_ref.at[pl.ds(0, 2 * (SLABS - 1))], grad_ref.at[pl.ds(0, 2 * (SLABS - 1))], recv_full
    ).wait()
    pltpu.make_async_copy(from_slab, from_slab, send_slab).wait()
    pltpu.make_async_copy(from_pencil, from_pencil, send_pencil).wait()
    pltpu.make_async_copy(
        from_pencil.at[pl.ds(0, PENCILS - 1), 0, pl.ds(0, 8), :],
        from_pencil.at[pl.ds(0, PENCILS - 1), 0, pl.ds(0, 8), :],
        send_grad,
    ).wait()
    pltpu.make_async_copy(
        grad_ref.at[pl.ds(0, 2 * (SLABS - 1))], grad_ref.at[pl.ds(0, 2 * (SLABS - 1))], send_full
    ).wait()


def exchange_call(part, weight, scale):
    vmem = pl.BlockSpec(memory_space=pltpu.VMEM)
    return pl.pallas_call(
        functools.partial(exchange_kernel, scale),
        out_shape=[
            jax.ShapeDtypeStruct((2, MODES, 2 * CHANNELS), f32),
            jax.ShapeDtypeStruct((KX, PAIRS, 2 * CHANNELS), bf16),
        ],
        in_specs=[vmem, vmem],
        out_specs=[vmem, vmem],
        scratch_shapes=[
            pltpu.VMEM((SLABS - 1, 2, 2, PAIRS, 2 * CHANNELS), bf16),
            pltpu.VMEM((2, 2, PAIRS, 2 * CHANNELS), f32),
            pltpu.VMEM((PENCILS - 1, 2, MODES, 2 * CHANNELS), f32),
            pltpu.VMEM((2, CHANNELS // 2 * MODES, 128), f32),
            pltpu.VMEM((MODES, 2 * CHANNELS), bf16),
        ]
        + [pltpu.SemaphoreType.DMA] * 8,
        compiler_params=pltpu.CompilerParams(
            collective_id=0, has_side_effects=True, vmem_limit_bytes=VMEM_LIMIT
        ),
        name="exchange",
    )(part, weight)


def build_sampler(grad_ref, sampler):
    eye = identity_matrix()

    def put(row, real, imag):
        sampler[row * 64 : row * 64 + 64, 0:PAIRS] = real.astype(bf16)
        sampler[row * 64 : row * 64 + 64, PAIRS:] = imag.astype(bf16)

    centre = flipped(grad_ref[HALF], eye)
    put(2 * HALF, centre[0:64], centre[64:128])
    for wave in range(1, HALF + 1):
        minus = flipped(grad_ref[HALF - wave], eye)
        if wave < HALF:
            plus = flipped(grad_ref[HALF + wave], eye)
            total, gap = plus + minus, plus - minus
        else:
            total, gap = minus, -minus
        put(wave - 1, total[0:64], total[64:128])
        put(HALF + wave - 1, gap[64:128], -gap[0:64])


def weight_gradient(spectrum_ref, out_ref, columns):
    lanes = lax.broadcasted_iota(jnp.int32, (MODES, 128), 1)
    spread_pair = jnp.where(
        lax.broadcasted_iota(jnp.int32, (128, 128), 0) % 2
        == lax.broadcasted_iota(jnp.int32, (128, 128), 1) // 64,
        1.0,
        0.0,
    ).astype(bf16)
    real, imag = spectrum_ref[0], spectrum_ref[1]
    g_real, g_imag = both_halves(real, True), both_halves(imag, True)
    for tile in range(CHANNELS // 2):
        keep = lanes // 2 == tile
        columns[0, tile * MODES : (tile + 1) * MODES] = jnp.where(keep, real, 0.0)
        columns[1, tile * MODES : (tile + 1) * MODES] = jnp.where(keep, imag, 0.0)
    f_real = split_product(columns[0], spread_pair)
    f_imag = split_product(columns[1], spread_pair)
    for tile in range(CHANNELS // 2):
        rows = slice(tile * MODES, (tile + 1) * MODES)
        where = slice(tile * 128, (tile + 1) * 128)
        out_ref[:, 0, where] = f_real[rows] * g_real + f_imag[rows] * g_imag
        out_ref[:, 1, where] = f_real[rows] * g_imag - f_imag[rows] * g_real


def sample_kernel(scale, chunk, grad_ref, spectrum_ref, pair_ref, lead_ref, out_ref, weight_out, sampler, columns):
    step = pl.program_id(0)

    @pl.when(step == 0)
    def _():
        build_sampler(grad_ref, sampler)
        weight_gradient(spectrum_ref, weight_out, columns)

    mixed = jnp.dot(sampler[...], pair_ref[...], preferred_element_type=f32)
    total = mixed[0:64] * lead_ref[0:1, :]
    for row in range(1, ROWS_L):
        total = total + mixed[row * 64 : (row + 1) * 64] * lead_ref[row : row + 1, :]
    out_ref[...] = total * scale


def sample_call(gradient, spectrum, pair, lead, scale):
    atoms = pair.shape[1]
    chunk = 1024
    return pl.pallas_call(
        functools.partial(sample_kernel, scale, chunk),
        grid=(atoms // chunk,),
        out_shape=[
            jax.ShapeDtypeStruct((CHANNELS, atoms), f32),
            jax.ShapeDtypeStruct((MODES, 2, CHANNELS * CHANNELS), f32),
        ],
        in_specs=[
            pl.BlockSpec((KX, PAIRS, 2 * CHANNELS), lambda i: (0, 0, 0)),
            pl.BlockSpec((2, MODES, 2 * CHANNELS), lambda i: (0, 0, 0)),
            pl.BlockSpec((2 * PAIRS, chunk), lambda i: (0, i)),
            pl.BlockSpec((ROWS_L_PAD, chunk), lambda i: (0, i)),
        ],
        out_specs=[
            pl.BlockSpec((CHANNELS, chunk), lambda i: (0, i)),
            pl.BlockSpec((MODES, 2, CHANNELS * CHANNELS), lambda i: (0, 0, 0)),
        ],
        scratch_shapes=[
            pltpu.VMEM((ROWS_L * 64, 2 * PAIRS), bf16),
            pltpu.VMEM((2, CHANNELS // 2 * MODES, 128), f32),
        ],
        compiler_params=pltpu.CompilerParams(vmem_limit_bytes=VMEM_LIMIT),
        name="sample",
    )(gradient, spectrum, pair, lead)


def on_device(features, cotangent, positions, tiles, weight):
    devices_all = lax.axis_size("slab") * lax.axis_size("pencil")
    scale = 1.0 / math.sqrt(TILES_DEV * TILE * devices_all)
    part, pair, lead = spread_call(features, cotangent, positions, tiles)
    spectrum, gradient = exchange_call(part, weight, scale)
    return tuple(sample_call(gradient, spectrum, pair, lead, scale))


def solution(mesh):
    return jax.shard_map(
        on_device,
        mesh=mesh,
        in_specs=(
            P(None, ("slab", "pencil")),
            P(None, ("slab", "pencil")),
            P(None, ("slab", "pencil")),
            P(("slab", "pencil")),
            P(("slab", "pencil"), None, None),
        ),
        out_specs=(P(None, ("slab", "pencil")), P(("slab", "pencil"), None, None)),
        check_vma=False,
    )
```

```python
import functools
import math

import jax
import jax.numpy as jnp
import numpy as np
from jax import lax
from jax.experimental import pallas as pl
from jax.experimental.pallas import tpu as pltpu
from jax.sharding import PartitionSpec as P

GRID = 256
KX = 16
KY = 16
KZ = 8
TILE = 128
TILES_DEV = 32
CHANNELS = 64
PAIRS = KY * KZ
HALF = KX // 2
ROWS_L = 2 * HALF + 1
ROWS_L_PAD = 24
STEP_FRACTION = 256
MODES = 16
CHIPS = 64
ODD, EVEN = (1, 3, 5, 7), (2, 4, 6, 8, 0)

bf16 = jnp.bfloat16
f32 = jnp.float32
last_last = (((1,), (1,)), ((), ()))
MESH_ID = pl.DeviceIdType.MESH
VMEM_LIMIT = 56 * 1024 * 1024


def spline_table(waves):
    basis = np.array(
        [[1, -3, 3, -1], [4, 0, -6, 3], [1, 3, 3, -3], [0, 0, 0, 1]], np.float64
    ) / 6.0
    turn = np.exp(-2j * np.pi * np.outer(waves, np.arange(4) - 1) / GRID)
    return turn @ basis


def column(values):
    rows = lax.broadcasted_iota(jnp.int32, (8, 1), 0)
    out = jnp.full((8, 1), float(values[0]), f32)
    for row in range(1, 8):
        out = jnp.where(rows == row, float(values[row]), out)
    return out


def axis_phase(position, first_wave):
    columns = position.shape[1]
    table = spline_table(np.arange(first_wave, first_wave + 8))
    wave = lax.broadcasted_iota(jnp.int32, (8, 1), 0) + first_wave
    cell = position // STEP_FRACTION
    fraction = (position % STEP_FRACTION).astype(f32) * (1.0 / STEP_FRACTION)
    turns = (wave * cell + GRID // 2) % GRID - GRID // 2
    half = turns.astype(f32) * (math.pi / GRID)
    square = half * half
    sine = -1.0 / 39916800.0
    for term in (1.0 / 362880.0, -1.0 / 5040.0, 1.0 / 120.0, -1.0 / 6.0, 1.0):
        sine = sine * square + term
    sine = sine * half
    cosine = 1.0 / 479001600.0
    for term in (-1.0 / 3628800.0, 1.0 / 40320.0, -1.0 / 720.0, 1.0 / 24.0, -0.5, 1.0):
        cosine = cosine * square + term
    turn_cos = 1.0 - 2.0 * sine * sine
    turn_sin = 2.0 * sine * cosine
    fraction = jnp.broadcast_to(fraction, (8, columns))
    stencil_real = column(table[:, 3].real)
    stencil_imag = column(table[:, 3].imag)
    for power in (2, 1, 0):
        stencil_real = stencil_real * fraction + column(table[:, power].real)
        stencil_imag = stencil_imag * fraction + column(table[:, power].imag)
    real = turn_cos * stencil_real + turn_sin * stencil_imag
    imag = turn_cos * stencil_imag - turn_sin * stencil_real
    return real, imag


def write_phases(position, live, lead_ref, pair_ref, where):
    lead_real, lead_imag = axis_phase(position[0:1], 1)
    side_real, side_imag = axis_phase(position[1:2], 1)
    depth_real, depth_imag = axis_phase(position[2:3], 0)
    lead_ref[0:8, where] = lead_real * live
    lead_ref[8:16, where] = lead_imag * live
    lead_ref[16:24, where] = jnp.broadcast_to(live, lead_real.shape)
    reals, imags = [None] * KY, [None] * KY
    reals[HALF], imags[HALF] = depth_real, depth_imag
    for wave in range(1, HALF + 1):
        real, imag = side_real[wave - 1 : wave], side_imag[wave - 1 : wave]
        rr, ii = real * depth_real, imag * depth_imag
        ri, ir = real * depth_imag, imag * depth_real
        if wave < HALF:
            reals[HALF + wave], imags[HALF + wave] = rr - ii, ri + ir
        reals[HALF - wave], imags[HALF - wave] = rr + ii, ri - ir
    for pair in range(HALF):
        rows = pl.ds(pair * 16, 16)
        pair_ref[rows, where] = jnp.concatenate(reals[2 * pair : 2 * pair + 2], 0).astype(bf16)
        rows = pl.ds(PAIRS + pair * 16, 16)
        pair_ref[rows, where] = jnp.concatenate(imags[2 * pair : 2 * pair + 2], 0).astype(bf16)


def identity_matrix():
    rows = lax.broadcasted_iota(jnp.int32, (128, 128), 0)
    columns = lax.broadcasted_iota(jnp.int32, (128, 128), 1)
    return jnp.where(rows == columns, 1.0, 0.0).astype(bf16)


def flipped(matrix, eye):
    return lax.dot_general(eye, matrix, last_last, preferred_element_type=f32)


def split_product(values, matrix):
    high = values.astype(bf16)
    low = (values - high.astype(f32)).astype(bf16)
    return jnp.dot(high, matrix, preferred_element_type=f32) + jnp.dot(
        low, matrix, preferred_element_type=f32
    )


def both_halves(values, upper):
    part = values[:, 64:128] if upper else values[:, 0:64]
    return jnp.concatenate([part, part], 1)


def rows_of(waves):
    nonzero = [wave for wave in waves if wave]
    rows = [wave - 1 for wave in nonzero] + [HALF + wave - 1 for wave in nonzero]
    return rows + [2 * HALF] * (len(waves) - len(nonzero))


def fused_kernel(
    scale,
    tiles_ref,
    pos_ref,
    cot_ref,
    feat_hbm,
    weight_hbm,
    out_ref,
    spectrum_ref,
    feat_ref,
    weight_ref,
    pair_ref,
    lead_ref,
    rows_ref,
    acc,
    part,
    from_mate,
    chip_sum,
    from_chip,
    products,
    own_block,
    grad_ref,
    sampler,
    load_sem,
    mate_send,
    mate_recv,
    chip_send,
    chip_recv,
    grad_send,
    grad_recv,
    both_send,
    both_recv,
):
    slab = lax.axis_index("slab")
    pencil = lax.axis_index("pencil")
    core = slab % 2
    level = slab // 2
    parity = pencil // 8
    place = pencil % 8
    mate = (level * 2 + 1 - core, pencil)
    atoms = pos_ref.shape[1]
    own_rows = pl.ds(pl.multiple_of(place * MODES, MODES), MODES)

    load_feat = pltpu.make_async_copy(feat_hbm, feat_ref, load_sem.at[0])
    load_weight = pltpu.make_async_copy(weight_hbm, weight_ref, load_sem.at[1])
    load_feat.start()
    load_weight.start()

    def chip_peer(step):
        chip = (level * 16 + pencil + step) % CHIPS
        return (chip // 16 * 2 + core, chip % 16)

    barrier = pltpu.get_barrier_semaphore()

    def greet(step, _):
        pl.semaphore_signal(barrier, inc=1, device_id=chip_peer(step), device_id_type=MESH_ID)
        return 0

    lax.fori_loop(1, CHIPS, greet, 0)
    pl.semaphore_signal(barrier, inc=1, device_id=mate, device_id_type=MESH_ID)

    sub = 512

    def phases(piece, _):
        where = pl.ds(pl.multiple_of(piece * sub, sub), sub)
        index = piece * sub + lax.broadcasted_iota(jnp.int32, (1, sub), 1)
        live = jnp.where(index < tiles_ref[0] * TILE, 1.0, 0.0).astype(f32)
        write_phases(pos_ref[:, where], live, lead_ref, pair_ref, where)
        return 0

    lax.fori_loop(0, atoms // sub, phases, 0)

    chunk = 2048

    def spread(values_ref, waves, base, first, last):
        rows = rows_of(waves)
        height = len(rows) * CHANNELS
        target = slice(base * CHANNELS, base * CHANNELS + height)

        def one(index, _):
            where = pl.ds(pl.multiple_of(index * chunk, chunk), chunk)
            values = values_ref[:, where].astype(f32)
            for place_of, row in enumerate(rows):
                rows_ref[place_of * 64 : place_of * 64 + 64, :] = (
                    values * lead_ref[row : row + 1, where]
                ).astype(bf16)
            acc[target, :] += lax.dot_general(
                rows_ref[0:height, :], pair_ref[:, where], last_last, preferred_element_type=f32
            )
            return 0

        if first == 0:
            acc[target, :] = jnp.zeros((height, 2 * PAIRS), f32)
        lax.fori_loop(first, last, one, 0)

    def finish(kind, waves, base):
        eye = identity_matrix()
        nonzero = [wave for wave in waves if wave]

        def put(index, real, imag):
            block = flipped(jnp.concatenate([real, imag], 0).astype(bf16), eye)
            part[kind, index // 4, index // 2 % 2, index % 2] = block.astype(bf16)

        def sums(slot):
            rows = slice((base + slot) * CHANNELS, (base + slot + 1) * CHANNELS)
            return acc[rows, 0:PAIRS], acc[rows, PAIRS:]

        for slot, wave in enumerate(nonzero):
            rr, ri = sums(slot)
            ir, ii = sums(len(nonzero) + slot)
            if wave < HALF:
                put(HALF + wave, rr - ii, ri + ir)
            put(HALF - wave, rr + ii, ri - ir)
        if 0 in waves:
            put(HALF, *sums(2 * len(nonzero)))

    def mate_copy(kind, side):
        return pltpu.make_async_remote_copy(
            src_ref=part.at[kind, :, 1 - core, side],
            dst_ref=from_mate.at[kind, side],
            send_sem=mate_send.at[kind, side],
            recv_sem=mate_recv.at[kind, side],
            device_id=mate,
            device_id_type=MESH_ID,
        )

    def to_owners(kind, side):
        mate_copy(kind, side).wait_recv()
        for height in range(4):
            total = part[kind, height, core, side].astype(f32) + from_mate[kind, side, height].astype(f32)
            chip_sum[kind, side, height] = total.astype(bf16)
        same = 1 - (parity + side) % 2

        def send(step, _):
            target_level = (level + step // 8) % 4
            target_place = (place + step) % 8
            pltpu.make_async_remote_copy(
                src_ref=chip_sum.at[
                    kind, side, target_level, pl.ds(pl.multiple_of(target_place * MODES, MODES), MODES), :
                ],
                dst_ref=from_chip.at[kind, step + 31 - 32 * same],
                send_sem=chip_send.at[kind],
                recv_sem=chip_recv.at[kind],
                device_id=(target_level * 2 + core, side * 8 + target_place),
                device_id_type=MESH_ID,
            ).start()
            return 0

        lax.fori_loop(same, 32, send, 0)

    def own_sum(kind):
        every = from_chip.at[kind]
        pltpu.make_async_copy(every, every, chip_recv.at[kind]).wait()
        total = chip_sum[kind, parity, level, own_rows, :].astype(f32)
        for source in range(CHIPS - 1):
            total = total + from_chip[kind, source].astype(f32)
        total = total * scale
        spectrum_ref[kind] = total
        return total

    def mix_and_share():
        total = own_sum(0)
        g_real, g_imag = both_halves(total, False), both_halves(total, True)
        lanes = lax.broadcasted_iota(jnp.int32, (MODES, 128), 1)
        halves = jnp.where(
            lax.broadcasted_iota(jnp.int32, (128, 128), 0) // 64
            == lax.broadcasted_iota(jnp.int32, (128, 128), 1) % 2,
            1.0,
            0.0,
        ).astype(bf16)
        for tile in range(CHANNELS // 2):
            w_real = weight_ref[:, 0, tile * 128 : (tile + 1) * 128]
            w_imag = weight_ref[:, 1, tile * 128 : (tile + 1) * 128]
            products[0, tile * MODES : (tile + 1) * MODES] = w_real * g_real + w_imag * g_imag
            products[1, tile * MODES : (tile + 1) * MODES] = w_real * g_imag - w_imag * g_real
        real_sums = split_product(products[0], halves)
        imag_sums = split_product(products[1], halves)
        block = jnp.zeros((MODES, 128), f32)
        for tile in range(CHANNELS // 2):
            rows = slice(tile * MODES, (tile + 1) * MODES)
            mixed = jnp.where(lanes < 64, real_sums[rows], imag_sums[rows])
            block = block + jnp.where(lanes % 64 // 2 == tile, mixed, 0.0)
        own_block[...] = block.astype(bf16)
        grad_ref[level, core, parity, own_rows, :] = block.astype(bf16)

        def share(step, _):
            pltpu.make_async_remote_copy(
                src_ref=own_block,
                dst_ref=grad_ref.at[level, core, parity, own_rows, :],
                send_sem=grad_send,
                recv_sem=grad_recv.at[parity],
                device_id=chip_peer(step),
                device_id_type=MESH_ID,
            ).start()
            return 0

        lax.fori_loop(1, CHIPS, share, 0)

    def both_copy(side):
        return pltpu.make_async_remote_copy(
            src_ref=grad_ref.at[:, core, side],
            dst_ref=grad_ref.at[:, core, side],
            send_sem=both_send.at[side],
            recv_sem=both_recv.at[side],
            device_id=mate,
            device_id_type=MESH_ID,
        )

    def forward(side):
        @pl.when(parity == side)
        def _():
            some = from_chip.at[0, pl.ds(0, 31)]
            pltpu.make_async_copy(some, some, grad_recv.at[side]).wait()

        @pl.when(parity != side)
        def _():
            some = from_chip.at[0, pl.ds(0, 32)]
            pltpu.make_async_copy(some, some, grad_recv.at[side]).wait()

        both_copy(side).start()

    def build_sampler(waves):
        eye = identity_matrix()
        nonzero = [wave for wave in waves if wave]

        def block(index):
            return flipped(grad_ref[index // 4, index // 2 % 2, index % 2], eye) * scale

        def put(slot, real, imag):
            sampler[slot * 64 : slot * 64 + 64, 0:PAIRS] = real.astype(bf16)
            sampler[slot * 64 : slot * 64 + 64, PAIRS:] = imag.astype(bf16)

        for slot, wave in enumerate(nonzero):
            minus = block(HALF - wave)
            if wave < HALF:
                plus = block(HALF + wave)
                total, gap = plus + minus, plus - minus
            else:
                total, gap = minus, -minus
            put(slot, total[0:64], total[64:128])
            put(len(nonzero) + slot, gap[64:128], -gap[0:64])
        if 0 in waves:
            centre = block(HALF)
            put(2 * len(nonzero), centre[0:64], centre[64:128])

    width = 1024

    def sample(waves, add, first, last):
        rows = rows_of(waves)

        def one(index, _):
            where = pl.ds(pl.multiple_of(index * width, width), width)
            mixed = jnp.dot(
                sampler[0 : len(rows) * 64, :], pair_ref[:, where], preferred_element_type=f32
            )
            total = out_ref[:, where] if add else 0.0
            for slot, row in enumerate(rows):
                total = total + mixed[slot * 64 : (slot + 1) * 64] * lead_ref[row : row + 1, where]
            out_ref[:, where] = total
            return 0

        lax.fori_loop(first, last, one, 0)

    steps = atoms // chunk
    spread(cot_ref, ODD, 0, 0, steps)
    finish(0, ODD, 0)
    pl.semaphore_wait(barrier, CHIPS)
    mate_copy(0, 1).start()
    spread(cot_ref, EVEN, 8, 0, steps)
    finish(0, EVEN, 8)
    mate_copy(0, 0).start()
    to_owners(0, 1)
    load_feat.wait()
    every_wave = ODD + EVEN
    spread(feat_ref, every_wave, 0, 0, 1)
    to_owners(0, 0)
    spread(feat_ref, every_wave, 0, 1, 3)
    load_weight.wait()

    @pl.when(parity == 1)
    def _():
        mix_and_share()

    spread(feat_ref, every_wave, 0, 3, steps)

    @pl.when(parity == 0)
    def _():
        mix_and_share()

    finish(1, every_wave, 0)
    mate_copy(1, 1).start()
    mate_copy(1, 0).start()
    forward(1)
    to_owners(1, 1)
    to_owners(1, 0)
    both_copy(1).wait_recv()
    build_sampler(ODD)
    half = atoms // width // 2
    sample(ODD, False, 0, half)
    forward(0)
    sample(ODD, False, half, 2 * half)
    both_copy(0).wait_recv()
    build_sampler(EVEN)
    sample(EVEN, True, 0, 2 * half)
    own_sum(1)
    for kind in range(2):
        for side in range(2):
            mate_copy(kind, side).wait_send()
        every = from_chip.at[kind]
        pltpu.make_async_copy(every, every, chip_send.at[kind]).wait()
    every = from_chip.at[0]
    pltpu.make_async_copy(every, every, grad_send).wait()
    both_copy(0).wait_send()
    both_copy(1).wait_send()


def fused_call(features, cotangent, positions, tiles, weight, scale):
    atoms = features.shape[1]
    vmem = pl.BlockSpec(memory_space=pltpu.VMEM)
    anywhere = pl.BlockSpec(memory_space=pl.ANY)
    return pl.pallas_call(
        functools.partial(fused_kernel, scale),
        out_shape=[
            jax.ShapeDtypeStruct((CHANNELS, atoms), f32),
            jax.ShapeDtypeStruct((2, MODES, 128), f32),
        ],
        in_specs=[pl.BlockSpec(memory_space=pltpu.SMEM), vmem, vmem, anywhere, anywhere],
        out_specs=[vmem, vmem],
        scratch_shapes=[
            pltpu.VMEM((CHANNELS, atoms), bf16),
            pltpu.VMEM(weight.shape, f32),
            pltpu.VMEM((2 * PAIRS, atoms), bf16),
            pltpu.VMEM((ROWS_L_PAD, atoms), f32),
            pltpu.VMEM((ROWS_L * CHANNELS, 2048), bf16),
            pltpu.VMEM((ROWS_L * CHANNELS, 2 * PAIRS), f32),
            pltpu.VMEM((2, 4, 2, 2, PAIRS, 128), bf16),
            pltpu.VMEM((2, 2, 4, PAIRS, 128), bf16),
            pltpu.VMEM((2, 2, 4, PAIRS, 128), bf16),
            pltpu.VMEM((2, CHIPS - 1, MODES, 128), bf16),
            pltpu.VMEM((2, CHANNELS // 2 * MODES, 128), f32),
            pltpu.VMEM((MODES, 128), bf16),
            pltpu.VMEM((4, 2, 2, PAIRS, 128), bf16),
            pltpu.VMEM((9 * CHANNELS, 2 * PAIRS), bf16),
            pltpu.SemaphoreType.DMA((2,)),
            pltpu.SemaphoreType.DMA((2, 2)),
            pltpu.SemaphoreType.DMA((2, 2)),
            pltpu.SemaphoreType.DMA((2,)),
            pltpu.SemaphoreType.DMA((2,)),
            pltpu.SemaphoreType.DMA,
            pltpu.SemaphoreType.DMA((2,)),
            pltpu.SemaphoreType.DMA((2,)),
            pltpu.SemaphoreType.DMA((2,)),
        ],
        compiler_params=pltpu.CompilerParams(
            collective_id=0, has_side_effects=True, vmem_limit_bytes=VMEM_LIMIT
        ),
        name="fused",
    )(tiles, positions, cotangent, features, weight)


def weight_kernel(spectrum_ref, out_ref, columns):
    lanes = lax.broadcasted_iota(jnp.int32, (MODES, 128), 1)
    spread_pair = jnp.where(
        lax.broadcasted_iota(jnp.int32, (128, 128), 0) % 2
        == lax.broadcasted_iota(jnp.int32, (128, 128), 1) // 64,
        1.0,
        0.0,
    ).astype(bf16)
    g_real, g_imag = both_halves(spectrum_ref[0], False), both_halves(spectrum_ref[0], True)
    real, imag = both_halves(spectrum_ref[1], False), both_halves(spectrum_ref[1], True)
    for tile in range(CHANNELS // 2):
        keep = lanes // 2 == tile
        columns[0, tile * MODES : (tile + 1) * MODES] = jnp.where(keep, real, 0.0)
        columns[1, tile * MODES : (tile + 1) * MODES] = jnp.where(keep, imag, 0.0)
    f_real = split_product(columns[0], spread_pair)
    f_imag = split_product(columns[1], spread_pair)
    for tile in range(CHANNELS // 2):
        rows = slice(tile * MODES, (tile + 1) * MODES)
        where = slice(tile * 128, (tile + 1) * 128)
        out_ref[:, 0, where] = f_real[rows] * g_real + f_imag[rows] * g_imag
        out_ref[:, 1, where] = f_real[rows] * g_imag - f_imag[rows] * g_real


def weight_call(spectrum):
    vmem = pl.BlockSpec(memory_space=pltpu.VMEM)
    return pl.pallas_call(
        weight_kernel,
        out_shape=jax.ShapeDtypeStruct((MODES, 2, CHANNELS * CHANNELS), f32),
        in_specs=[vmem],
        out_specs=vmem,
        scratch_shapes=[pltpu.VMEM((2, CHANNELS // 2 * MODES, 128), f32)],
        compiler_params=pltpu.CompilerParams(vmem_limit_bytes=16 * 1024 * 1024),
        name="weight_gradient",
    )(spectrum)


def on_device(features, cotangent, positions, tiles, weight):
    devices_all = lax.axis_size("slab") * lax.axis_size("pencil")
    scale = 1.0 / math.sqrt(TILES_DEV * TILE * devices_all)
    gradient, spectrum = fused_call(features, cotangent, positions, tiles, weight, scale)
    return gradient, weight_call(spectrum)


def solution(mesh):
    return jax.shard_map(
        on_device,
        mesh=mesh,
        in_specs=(
            P(None, ("slab", "pencil")),
            P(None, ("slab", "pencil")),
            P(None, ("slab", "pencil")),
            P(("slab", "pencil")),
            P(("slab", "pencil"), None, None),
        ),
        out_specs=(P(None, ("slab", "pencil")), P(("slab", "pencil"), None, None)),
        check_vma=False,
    )
```

```python
import functools
import math

import jax
import jax.numpy as jnp
import numpy as np
from jax import lax
from jax.experimental import pallas as pl
from jax.experimental.pallas import tpu as pltpu
from jax.sharding import PartitionSpec as P

GRID = 256
KX = 16
KY = 16
KZ = 8
TILE = 128
TILES_DEV = 32
CHANNELS = 64
PAIRS = KY * KZ
HALF = KX // 2
ROWS_L = 2 * HALF + 1
ROWS_L_PAD = 24
STEP_FRACTION = 256
MODES = 16
CHIPS = 64
ODD, EVEN = (1, 3, 5, 7), (2, 4, 6, 8, 0)

bf16 = jnp.bfloat16
f32 = jnp.float32
last_last = (((1,), (1,)), ((), ()))
MESH_ID = pl.DeviceIdType.MESH
VMEM_LIMIT = 56 * 1024 * 1024


def spline_table(waves):
    basis = np.array(
        [[1, -3, 3, -1], [4, 0, -6, 3], [1, 3, 3, -3], [0, 0, 0, 1]], np.float64
    ) / 6.0
    turn = np.exp(-2j * np.pi * np.outer(waves, np.arange(4) - 1) / GRID)
    return turn @ basis


def column(values):
    rows = lax.broadcasted_iota(jnp.int32, (8, 1), 0)
    out = jnp.full((8, 1), float(values[0]), f32)
    for row in range(1, 8):
        out = jnp.where(rows == row, float(values[row]), out)
    return out


def axis_phase(position, first_wave):
    columns = position.shape[1]
    table = spline_table(np.arange(first_wave, first_wave + 8))
    wave = lax.broadcasted_iota(jnp.int32, (8, 1), 0) + first_wave
    cell = position >> 8
    fraction = (position & (STEP_FRACTION - 1)).astype(f32) * (1.0 / STEP_FRACTION)
    turns = ((wave * cell + GRID // 2) & (GRID - 1)) - GRID // 2
    half = turns.astype(f32) * (math.pi / GRID)
    square = half * half
    sine = -1.0 / 39916800.0
    for term in (1.0 / 362880.0, -1.0 / 5040.0, 1.0 / 120.0, -1.0 / 6.0, 1.0):
        sine = sine * square + term
    sine = sine * half
    cosine = 1.0 / 479001600.0
    for term in (-1.0 / 3628800.0, 1.0 / 40320.0, -1.0 / 720.0, 1.0 / 24.0, -0.5, 1.0):
        cosine = cosine * square + term
    turn_cos = 1.0 - 2.0 * sine * sine
    turn_sin = 2.0 * sine * cosine
    fraction = jnp.broadcast_to(fraction, (8, columns))
    stencil_real = column(table[:, 3].real)
    stencil_imag = column(table[:, 3].imag)
    for power in (2, 1, 0):
        stencil_real = stencil_real * fraction + column(table[:, power].real)
        stencil_imag = stencil_imag * fraction + column(table[:, power].imag)
    real = turn_cos * stencil_real + turn_sin * stencil_imag
    imag = turn_cos * stencil_imag - turn_sin * stencil_real
    return real, imag


def write_phases(position, live, lead_ref, pair_ref, where):
    lead_real, lead_imag = axis_phase(position[0:1], 1)
    side_real, side_imag = axis_phase(position[1:2], 1)
    depth_real, depth_imag = axis_phase(position[2:3], 0)
    lead_ref[0:8, where] = lead_real * live
    lead_ref[8:16, where] = lead_imag * live
    lead_ref[16:24, where] = jnp.broadcast_to(live, lead_real.shape)
    reals, imags = [None] * KY, [None] * KY
    reals[HALF], imags[HALF] = depth_real, depth_imag
    for wave in range(1, HALF + 1):
        real, imag = side_real[wave - 1 : wave], side_imag[wave - 1 : wave]
        rr, ii = real * depth_real, imag * depth_imag
        ri, ir = real * depth_imag, imag * depth_real
        if wave < HALF:
            reals[HALF + wave], imags[HALF + wave] = rr - ii, ri + ir
        reals[HALF - wave], imags[HALF - wave] = rr + ii, ri - ir
    for pair in range(HALF):
        rows = pl.ds(pair * 16, 16)
        pair_ref[rows, where] = jnp.concatenate(reals[2 * pair : 2 * pair + 2], 0).astype(bf16)
        rows = pl.ds(PAIRS + pair * 16, 16)
        pair_ref[rows, where] = jnp.concatenate(imags[2 * pair : 2 * pair + 2], 0).astype(bf16)


def identity_matrix():
    rows = lax.broadcasted_iota(jnp.int32, (128, 128), 0)
    columns = lax.broadcasted_iota(jnp.int32, (128, 128), 1)
    return jnp.where(rows == columns, 1.0, 0.0).astype(bf16)


def flipped(matrix, eye):
    return lax.dot_general(eye, matrix, last_last, preferred_element_type=f32)


TILE_ROWS = CHANNELS // 2 * MODES


def put_split(products, side, tile, values):
    high = values.astype(bf16)
    rows = pl.ds((2 * side * CHANNELS // 2 + tile) * MODES, MODES)
    products[rows, :] = high
    rows = pl.ds(((2 * side + 1) * CHANNELS // 2 + tile) * MODES, MODES)
    products[rows, :] = (values - high.astype(f32)).astype(bf16)


def split_sums(products, matrix):
    every = jnp.dot(products[...], matrix, preferred_element_type=f32)
    parts = [every[index * TILE_ROWS : (index + 1) * TILE_ROWS] for index in range(4)]
    return parts[0] + parts[1], parts[2] + parts[3]


def both_halves(values, upper):
    part = values[:, 64:128] if upper else values[:, 0:64]
    return jnp.concatenate([part, part], 1)


def rows_of(waves):
    rows = []
    for wave in waves:
        rows += [wave - 1, HALF + wave - 1] if wave else [2 * HALF]
    return rows


def weight_gradient(g_sum, f_sum, weight_out, products):
    lanes = lax.broadcasted_iota(jnp.int32, (MODES, 128), 1)
    spread_pair = jnp.where(
        lax.broadcasted_iota(jnp.int32, (128, 128), 0) % 2
        == lax.broadcasted_iota(jnp.int32, (128, 128), 1) // 64,
        1.0,
        0.0,
    ).astype(bf16)
    g_real, g_imag = both_halves(g_sum, False), both_halves(g_sum, True)
    real, imag = both_halves(f_sum, False), both_halves(f_sum, True)
    for tile in range(CHANNELS // 2):
        keep = lanes // 2 == tile
        put_split(products, 0, tile, jnp.where(keep, real, 0.0))
        put_split(products, 1, tile, jnp.where(keep, imag, 0.0))
    f_real, f_imag = split_sums(products, spread_pair)
    for tile in range(CHANNELS // 2):
        rows = slice(tile * MODES, (tile + 1) * MODES)
        where = slice(tile * 128, (tile + 1) * 128)
        weight_out[:, 0, where] = f_real[rows] * g_real + f_imag[rows] * g_imag
        weight_out[:, 1, where] = f_real[rows] * g_imag - f_imag[rows] * g_real


def sampled(waves, sampler, pair, lead):
    rows = rows_of(waves)
    mixed = jnp.dot(sampler, pair, preferred_element_type=f32)
    total = 0.0
    for slot, row in enumerate(rows):
        total = total + mixed[slot * 64 : (slot + 1) * 64] * lead[row : row + 1]
    return total


def fused_kernel(
    scale,
    tiles_ref,
    pos_ref,
    cot_hbm,
    feat_hbm,
    weight_hbm,
    weight_out,
    even_sampler,
    out_hbm,
    pair_hbm,
    lead_hbm,
    cot_ref,
    feat_ref,
    weight_ref,
    weight_tiles,
    pair_ref,
    lead_ref,
    rows_ref,
    acc,
    out_ref,
    part,
    from_mate,
    chip_sum,
    from_chip,
    products,
    own_block,
    grad_ref,
    odd_sampler,
    g_sum,
    load_sem,
    store_sem,
    mate_send,
    mate_recv,
    chip_send,
    chip_recv,
    grad_send,
    grad_recv,
    both_send,
    both_recv,
):
    slab = lax.axis_index("slab")
    pencil = lax.axis_index("pencil")
    core = slab % 2
    level = slab // 2
    parity = pencil // 8
    place = pencil % 8
    mate = (level * 2 + 1 - core, pencil)
    atoms = pos_ref.shape[1]
    own_rows = pl.ds(pl.multiple_of(place * MODES, MODES), MODES)

    load_cot = pltpu.make_async_copy(cot_hbm, cot_ref, load_sem.at[2])
    load_cot.start()
    load_feat = pltpu.make_async_copy(feat_hbm, feat_ref, load_sem.at[0])
    load_weight = pltpu.make_async_copy(weight_hbm, weight_ref, load_sem.at[1])
    load_feat.start()
    load_weight.start()

    def chip_peer(step):
        chip = (level * 16 + pencil + step + 1) % CHIPS
        return (chip // 16 * 2 + core, chip % 16)

    barrier = pltpu.get_barrier_semaphore()

    def greet(step, _):
        pl.semaphore_signal(barrier, inc=1, device_id=chip_peer(step), device_id_type=MESH_ID)
        return 0

    lax.fori_loop(0, CHIPS - 1, greet, 0)
    pl.semaphore_signal(barrier, inc=1, device_id=mate, device_id_type=MESH_ID)

    sub = 512
    chunk = 2048

    def phases(index):
        for piece in range(chunk // sub):
            start = index * chunk + piece * sub
            where = slice(start, start + sub)
            atom = start + lax.broadcasted_iota(jnp.int32, (1, sub), 1)
            live = jnp.where(atom < tiles_ref[0] * TILE, 1.0, 0.0).astype(f32)
            write_phases(pos_ref[:, where], live, lead_ref, pair_ref, where)

    def spread(values_ref, waves, base, where, add=False):
        rows = rows_of(waves)
        height = len(rows) * CHANNELS
        target = slice(base * CHANNELS, base * CHANNELS + height)
        values = values_ref[:, where].astype(f32)
        for slot, row in enumerate(rows):
            rows_ref[slot * 64 : slot * 64 + 64, where] = (
                values * lead_ref[row : row + 1, where]
            ).astype(bf16)
        product = lax.dot_general(
            pair_ref[:, where], rows_ref[0:height, where], last_last, preferred_element_type=f32
        )
        acc[:, target] = acc[:, target] + product if add else product

    def finish(kind, waves, base):
        sign = jnp.where(lax.broadcasted_iota(jnp.int32, (PAIRS, 128), 1) < CHANNELS, -1.0, 1.0)

        def put(index, block):
            part[kind, index // 4, index // 2 % 2, index % 2] = block.astype(bf16)

        for slot, wave in enumerate(waves):
            start = (base + 2 * slot) * CHANNELS
            if wave == 0:
                where = slice(start, start + CHANNELS)
                put(HALF, jnp.concatenate([acc[0:PAIRS, where], acc[PAIRS:, where]], 1))
                continue
            where = slice(start, start + 128)
            straight = acc[0:PAIRS, where]
            crossed = pltpu.roll(acc[PAIRS:, where], CHANNELS, 1)
            if wave < HALF:
                put(HALF + wave, straight + sign * crossed)
            put(HALF - wave, crossed - sign * straight)

    def mate_copy(kind, side):
        return pltpu.make_async_remote_copy(
            src_ref=part.at[kind, :, 1 - core, side],
            dst_ref=from_mate.at[kind, side],
            send_sem=mate_send.at[kind, side],
            recv_sem=mate_recv.at[kind, side],
            device_id=mate,
            device_id_type=MESH_ID,
        )

    def to_owners(kind, side):
        mate_copy(kind, side).wait_recv()
        for height in range(4):
            total = part[kind, height, core, side].astype(f32) + from_mate[kind, side, height].astype(f32)
            chip_sum[kind, side, height] = total.astype(bf16)
        same = 1 - (parity + side) % 2

        def send(step, _):
            ahead = step + same
            target_level = (level + ahead // 8) % 4
            target_place = (place + ahead) % 8
            pltpu.make_async_remote_copy(
                src_ref=chip_sum.at[
                    kind, side, target_level, pl.ds(pl.multiple_of(target_place * MODES, MODES), MODES), :
                ],
                dst_ref=from_chip.at[kind, step + 31 - 31 * same],
                send_sem=chip_send.at[kind],
                recv_sem=chip_recv.at[kind],
                device_id=(target_level * 2 + core, side * 8 + target_place),
                device_id_type=MESH_ID,
            ).start()
            return 0

        lax.fori_loop(0, 32 - same, send, 0)

    def own_sum(kind):
        every = from_chip.at[kind]
        pltpu.make_async_copy(every, every, chip_recv.at[kind]).wait()
        total = chip_sum[kind, parity, level, own_rows, :].astype(f32)
        for source in range(CHIPS - 1):
            total = total + from_chip[kind, source].astype(f32)
        return total * scale

    def lay_weights():
        load_weight.wait()
        for tile in range(CHANNELS // 2):
            for side in range(2):
                weight_tiles[side, tile] = weight_ref[:, side, tile * 128 : (tile + 1) * 128]

    def mix_and_share():
        total = own_sum(0)
        g_sum[...] = total
        g_real, g_imag = both_halves(total, False), both_halves(total, True)
        lanes = lax.broadcasted_iota(jnp.int32, (MODES, 128), 1)
        halves = jnp.where(
            lax.broadcasted_iota(jnp.int32, (128, 128), 0) // 64
            == lax.broadcasted_iota(jnp.int32, (128, 128), 1) % 2,
            1.0,
            0.0,
        ).astype(bf16)
        for tile in range(CHANNELS // 2):
            w_real = weight_tiles[0, tile]
            w_imag = weight_tiles[1, tile]
            put_split(products, 0, tile, w_real * g_real + w_imag * g_imag)
            put_split(products, 1, tile, w_real * g_imag - w_imag * g_real)
        real_sums, imag_sums = split_sums(products, halves)
        block = jnp.zeros((MODES, 128), f32)
        for tile in range(CHANNELS // 2):
            rows = slice(tile * MODES, (tile + 1) * MODES)
            mixed = jnp.where(lanes < 64, real_sums[rows], imag_sums[rows])
            block = block + jnp.where(lanes % 64 // 2 == tile, mixed, 0.0)
        own_block[...] = block.astype(bf16)
        grad_ref[parity, level, core, own_rows, :] = block.astype(bf16)

        def share(step, _):
            pltpu.make_async_remote_copy(
                src_ref=own_block,
                dst_ref=grad_ref.at[parity, level, core, own_rows, :],
                send_sem=grad_send,
                recv_sem=grad_recv.at[parity],
                device_id=chip_peer(step),
                device_id_type=MESH_ID,
            ).start()
            return 0

        lax.fori_loop(0, CHIPS - 1, share, 0)

    def both_copy(side):
        return pltpu.make_async_remote_copy(
            src_ref=grad_ref.at[side, :, core],
            dst_ref=grad_ref.at[side, :, core],
            send_sem=both_send.at[side],
            recv_sem=both_recv.at[side],
            device_id=mate,
            device_id_type=MESH_ID,
        )

    def forward(side):
        @pl.when(parity == side)
        def _():
            some = from_chip.at[0, pl.ds(0, 31)]
            pltpu.make_async_copy(some, some, grad_recv.at[side]).wait()

        @pl.when(parity != side)
        def _():
            some = from_chip.at[0, pl.ds(0, 32)]
            pltpu.make_async_copy(some, some, grad_recv.at[side]).wait()

        both_copy(side).start()

    def build_sampler(side, waves, sampler):
        blocks = flipped(grad_ref[side].reshape(8 * PAIRS, 128), identity_matrix())

        def block(index):
            return blocks[:, index // 2 * PAIRS : (index // 2 + 1) * PAIRS] * scale

        def put(slot, real, imag):
            sampler[slot * 64 : slot * 64 + 64, 0:PAIRS] = real.astype(bf16)
            sampler[slot * 64 : slot * 64 + 64, PAIRS:] = imag.astype(bf16)

        for slot, wave in enumerate(waves):
            minus = block(HALF - wave)
            if wave == 0:
                put(2 * slot, minus[0:64], minus[64:128])
                continue
            if wave < HALF:
                plus = block(HALF + wave)
                total, gap = plus + minus, plus - minus
            else:
                total, gap = minus, -minus
            put(2 * slot, total[0:64], total[64:128])
            put(2 * slot + 1, gap[64:128], -gap[0:64])

    width = 2048

    def store_out(index):
        where = pl.ds(pl.multiple_of(index * width, width), width)
        return pltpu.make_async_copy(out_ref.at[:, where], out_hbm.at[:, where], store_sem.at[index + 2])

    def sample(index):
        where = slice(index * width, (index + 1) * width)
        out_ref[:, where] = sampled(ODD, odd_sampler[...], pair_ref[:, where], lead_ref[:, where])
        store_out(index).start()

    phases(0)
    load_cot.wait()
    for index in range(atoms // chunk):
        if index + 1 < atoms // chunk:
            phases(index + 1)
        spread(cot_ref, ODD, 0, slice(index * chunk, (index + 1) * chunk), index > 0)
    finish(0, ODD, 0)
    pl.semaphore_wait(barrier, CHIPS)
    mate_copy(0, 1).start()
    store_pair = pltpu.make_async_copy(pair_ref, pair_hbm, store_sem.at[0])
    store_lead = pltpu.make_async_copy(lead_ref, lead_hbm, store_sem.at[1])
    store_pair.start()
    store_lead.start()
    whole = slice(0, atoms)
    low, high = EVEN[:2], EVEN[2:]
    spread(cot_ref, low, 8, whole)
    to_owners(0, 1)
    spread(cot_ref, high, 12, whole)
    finish(0, low, 8)
    finish(0, high, 12)
    mate_copy(0, 0).start()
    load_feat.wait()
    spread(feat_ref, ODD[:2], 0, whole)
    to_owners(0, 0)
    spread(feat_ref, ODD[2:], 4, whole)
    lay_weights()
    spread(feat_ref, low, 8, whole)

    @pl.when(parity == 1)
    def _():
        mix_and_share()

    spread(feat_ref, high, 12, whole)
    finish(1, ODD[:2], 0)
    finish(1, ODD[2:], 4)
    finish(1, low, 8)
    finish(1, high, 12)
    mate_copy(1, 1).start()
    mate_copy(1, 0).start()

    @pl.when(parity == 0)
    def _():
        mix_and_share()

    to_owners(1, 1)
    to_owners(1, 0)
    forward(1)
    both_copy(1).wait_recv()
    build_sampler(1, ODD, odd_sampler)
    count = atoms // width
    for index in range(count // 2):
        sample(index)
    forward(0)
    for index in range(count // 2, count):
        sample(index)
    weight_gradient(g_sum[...], own_sum(1), weight_out, products)
    both_copy(0).wait_recv()
    build_sampler(0, EVEN, even_sampler)
    for kind in range(2):
        for side in range(2):
            mate_copy(kind, side).wait_send()
        every = from_chip.at[kind]
        pltpu.make_async_copy(every, every, chip_send.at[kind]).wait()
    every = from_chip.at[0]
    pltpu.make_async_copy(every, every, grad_send).wait()
    both_copy(0).wait_send()
    both_copy(1).wait_send()
    store_pair.wait()
    store_lead.wait()
    for index in range(count):
        store_out(index).wait()


def fused_call(features, cotangent, positions, tiles, weight, scale):
    atoms = features.shape[1]
    vmem = pl.BlockSpec(memory_space=pltpu.VMEM)
    anywhere = pl.BlockSpec(memory_space=pl.ANY)
    return pl.pallas_call(
        functools.partial(fused_kernel, scale),
        out_shape=[
            jax.ShapeDtypeStruct(weight.shape, f32),
            jax.ShapeDtypeStruct((9 * CHANNELS, 2 * PAIRS), bf16),
            jax.ShapeDtypeStruct((CHANNELS, atoms), f32),
            jax.ShapeDtypeStruct((2 * PAIRS, atoms), bf16),
            jax.ShapeDtypeStruct((ROWS_L_PAD, atoms), f32),
        ],
        in_specs=[pl.BlockSpec(memory_space=pltpu.SMEM), vmem, anywhere, anywhere, anywhere],
        out_specs=[vmem, vmem, anywhere, anywhere, anywhere],
        scratch_shapes=[
            pltpu.VMEM((CHANNELS, atoms), bf16),
            pltpu.VMEM((CHANNELS, atoms), bf16),
            pltpu.VMEM(weight.shape, f32),
            pltpu.VMEM((2, CHANNELS // 2, MODES, 128), f32),
            pltpu.VMEM((2 * PAIRS, atoms), bf16),
            pltpu.VMEM((ROWS_L_PAD, atoms), f32),
            pltpu.VMEM((9 * CHANNELS, atoms), bf16),
            pltpu.VMEM((2 * PAIRS, (ROWS_L + 1) * CHANNELS), f32),
            pltpu.VMEM((CHANNELS, atoms), f32),
            pltpu.VMEM((2, 4, 2, 2, PAIRS, 128), bf16),
            pltpu.VMEM((2, 2, 4, PAIRS, 128), bf16),
            pltpu.VMEM((2, 2, 4, PAIRS, 128), bf16),
            pltpu.VMEM((2, CHIPS - 1, MODES, 128), bf16),
            pltpu.VMEM((4 * TILE_ROWS, 128), bf16),
            pltpu.VMEM((MODES, 128), bf16),
            pltpu.VMEM((2, 4, 2, PAIRS, 128), bf16),
            pltpu.VMEM((8 * CHANNELS, 2 * PAIRS), bf16),
            pltpu.VMEM((MODES, 128), f32),
            pltpu.SemaphoreType.DMA((3,)),
            pltpu.SemaphoreType.DMA((6,)),
            pltpu.SemaphoreType.DMA((2, 2)),
            pltpu.SemaphoreType.DMA((2, 2)),
            pltpu.SemaphoreType.DMA((2,)),
            pltpu.SemaphoreType.DMA((2,)),
            pltpu.SemaphoreType.DMA,
            pltpu.SemaphoreType.DMA((2,)),
            pltpu.SemaphoreType.DMA((2,)),
            pltpu.SemaphoreType.DMA((2,)),
        ],
        compiler_params=pltpu.CompilerParams(
            collective_id=0, has_side_effects=True, vmem_limit_bytes=VMEM_LIMIT
        ),
        name="fused",
    )(tiles, positions, cotangent, features, weight)


def last_kernel(
    weight_in, sampler_ref, pair_ref, lead_ref, part_ref, out_ref, weight_out, weight_ref, load_sem, store_sem
):
    step = pl.program_id(0)
    load = pltpu.make_async_copy(weight_in, weight_ref, load_sem)
    store = pltpu.make_async_copy(weight_ref, weight_out, store_sem)

    @pl.when(step == 0)
    def _():
        load.start()

    @pl.when(step == 1)
    def _():
        load.wait()
        store.start()

    out_ref[...] = part_ref[...] + sampled(EVEN, sampler_ref[...], pair_ref[...], lead_ref[...])

    @pl.when(step == pl.num_programs(0) - 1)
    def _():
        store.wait()


def last_call(weight_gradient_here, sampler, out, pair, lead):
    atoms = pair.shape[1]
    width = 2048
    return pl.pallas_call(
        last_kernel,
        grid=(atoms // width,),
        out_shape=[
            jax.ShapeDtypeStruct((CHANNELS, atoms), f32),
            jax.ShapeDtypeStruct(weight_gradient_here.shape, f32),
        ],
        in_specs=[
            pl.BlockSpec(memory_space=pl.ANY),
            pl.BlockSpec((9 * CHANNELS, 2 * PAIRS), lambda i: (0, 0)),
            pl.BlockSpec((2 * PAIRS, width), lambda i: (0, i)),
            pl.BlockSpec((ROWS_L_PAD, width), lambda i: (0, i)),
            pl.BlockSpec((CHANNELS, width), lambda i: (0, i)),
        ],
        out_specs=[
            pl.BlockSpec((CHANNELS, width), lambda i: (0, i)),
            pl.BlockSpec(memory_space=pl.ANY),
        ],
        scratch_shapes=[
            pltpu.VMEM(weight_gradient_here.shape, f32),
            pltpu.SemaphoreType.DMA,
            pltpu.SemaphoreType.DMA,
        ],
        compiler_params=pltpu.CompilerParams(vmem_limit_bytes=VMEM_LIMIT),
        name="last",
    )(weight_gradient_here, sampler, pair, lead, out)


def on_device(features, cotangent, positions, tiles, weight):
    devices_all = lax.axis_size("slab") * lax.axis_size("pencil")
    scale = 1.0 / math.sqrt(TILES_DEV * TILE * devices_all)
    fused = fused_call(features, cotangent, positions, tiles, weight, scale)
    return tuple(last_call(*fused))


def solution(mesh):
    return jax.shard_map(
        on_device,
        mesh=mesh,
        in_specs=(
            P(None, ("slab", "pencil")),
            P(None, ("slab", "pencil")),
            P(None, ("slab", "pencil")),
            P(("slab", "pencil")),
            P(("slab", "pencil"), None, None),
        ),
        out_specs=(P(None, ("slab", "pencil")), P(("slab", "pencil"), None, None)),
        check_vma=False,
    )
```

```python
import functools
import math

import jax
import jax.numpy as jnp
import numpy as np
from jax import lax
from jax.experimental import pallas as pl
from jax.experimental.pallas import tpu as pltpu
from jax.sharding import PartitionSpec as P

GRID = 256
KX = 16
KY = 16
KZ = 8
TILE = 128
TILES_DEV = 32
CHANNELS = 64
PAIRS = KY * KZ
HALF = KX // 2
ROWS_L = 2 * HALF + 1
ROWS_L_PAD = 24
STEP_FRACTION = 256
MODES = 16
CHIPS = 64
ODD, EVEN = (1, 3, 5, 7), (2, 4, 6, 8, 0)

bf16 = jnp.bfloat16
f32 = jnp.float32
last_last = (((1,), (1,)), ((), ()))
MESH_ID = pl.DeviceIdType.MESH
VMEM_LIMIT = 56 * 1024 * 1024


def spline_table(waves):
    basis = np.array(
        [[1, -3, 3, -1], [4, 0, -6, 3], [1, 3, 3, -3], [0, 0, 0, 1]], np.float64
    ) / 6.0
    turn = np.exp(-2j * np.pi * np.outer(waves, np.arange(4) - 1) / GRID)
    return turn @ basis


def column(values):
    rows = lax.broadcasted_iota(jnp.int32, (8, 1), 0)
    out = jnp.full((8, 1), float(values[0]), f32)
    for row in range(1, 8):
        out = jnp.where(rows == row, float(values[row]), out)
    return out


def axis_phase(position, first_wave):
    columns = position.shape[1]
    table = spline_table(np.arange(first_wave, first_wave + 8))
    wave = lax.broadcasted_iota(jnp.int32, (8, 1), 0) + first_wave
    cell = position >> 8
    fraction = (position & (STEP_FRACTION - 1)).astype(f32) * (1.0 / STEP_FRACTION)
    turns = ((wave * cell + GRID // 2) & (GRID - 1)) - GRID // 2
    half = turns.astype(f32) * (math.pi / GRID)
    square = half * half
    sine = -1.0 / 39916800.0
    for term in (1.0 / 362880.0, -1.0 / 5040.0, 1.0 / 120.0, -1.0 / 6.0, 1.0):
        sine = sine * square + term
    sine = sine * half
    cosine = 1.0 / 479001600.0
    for term in (-1.0 / 3628800.0, 1.0 / 40320.0, -1.0 / 720.0, 1.0 / 24.0, -0.5, 1.0):
        cosine = cosine * square + term
    turn_cos = 1.0 - 2.0 * sine * sine
    turn_sin = 2.0 * sine * cosine
    fraction = jnp.broadcast_to(fraction, (8, columns))
    stencil_real = column(table[:, 3].real)
    stencil_imag = column(table[:, 3].imag)
    for power in (2, 1, 0):
        stencil_real = stencil_real * fraction + column(table[:, power].real)
        stencil_imag = stencil_imag * fraction + column(table[:, power].imag)
    real = turn_cos * stencil_real + turn_sin * stencil_imag
    imag = turn_cos * stencil_imag - turn_sin * stencil_real
    return real, imag


def write_phases(position, live, lead_ref, pair_ref, where):
    lead_real, lead_imag = axis_phase(position[0:1], 1)
    side_real, side_imag = axis_phase(position[1:2], 1)
    depth_real, depth_imag = axis_phase(position[2:3], 0)
    lead_ref[0:8, where] = lead_real * live
    lead_ref[8:16, where] = lead_imag * live
    lead_ref[16:24, where] = jnp.broadcast_to(live, lead_real.shape)
    reals, imags = [None] * KY, [None] * KY
    reals[HALF], imags[HALF] = depth_real, depth_imag
    for wave in range(1, HALF + 1):
        real, imag = side_real[wave - 1 : wave], side_imag[wave - 1 : wave]
        rr, ii = real * depth_real, imag * depth_imag
        ri, ir = real * depth_imag, imag * depth_real
        if wave < HALF:
            reals[HALF + wave], imags[HALF + wave] = rr - ii, ri + ir
        reals[HALF - wave], imags[HALF - wave] = rr + ii, ri - ir
    for pair in range(HALF):
        rows = pl.ds(pair * 16, 16)
        pair_ref[rows, where] = jnp.concatenate(reals[2 * pair : 2 * pair + 2], 0).astype(bf16)
        rows = pl.ds(PAIRS + pair * 16, 16)
        pair_ref[rows, where] = jnp.concatenate(imags[2 * pair : 2 * pair + 2], 0).astype(bf16)


def identity_matrix():
    rows = lax.broadcasted_iota(jnp.int32, (128, 128), 0)
    columns = lax.broadcasted_iota(jnp.int32, (128, 128), 1)
    return jnp.where(rows == columns, 1.0, 0.0).astype(bf16)


def flipped(matrix, eye):
    return lax.dot_general(eye, matrix, last_last, preferred_element_type=f32)


TILE_ROWS = CHANNELS // 2 * MODES


def put_split(products, side, tile, values):
    high = values.astype(bf16)
    rows = pl.ds((2 * side * CHANNELS // 2 + tile) * MODES, MODES)
    products[rows, :] = high
    rows = pl.ds(((2 * side + 1) * CHANNELS // 2 + tile) * MODES, MODES)
    products[rows, :] = (values - high.astype(f32)).astype(bf16)


def split_sums(products, matrix):
    every = jnp.dot(products[...], matrix, preferred_element_type=f32)
    parts = [every[index * TILE_ROWS : (index + 1) * TILE_ROWS] for index in range(4)]
    return parts[0] + parts[1], parts[2] + parts[3]


def both_halves(values, upper):
    part = values[:, 64:128] if upper else values[:, 0:64]
    return jnp.concatenate([part, part], 1)


def rows_of(waves):
    rows = []
    for wave in waves:
        rows += [wave - 1, HALF + wave - 1] if wave else [2 * HALF]
    return rows


def weight_gradient(g_sum, f_sum, weight_out, products):
    lanes = lax.broadcasted_iota(jnp.int32, (MODES, 128), 1)
    spread_pair = jnp.where(
        lax.broadcasted_iota(jnp.int32, (128, 128), 0) % 2
        == lax.broadcasted_iota(jnp.int32, (128, 128), 1) // 64,
        1.0,
        0.0,
    ).astype(bf16)
    g_real, g_imag = both_halves(g_sum, False), both_halves(g_sum, True)
    real, imag = both_halves(f_sum, False), both_halves(f_sum, True)
    for tile in range(CHANNELS // 2):
        keep = lanes // 2 == tile
        put_split(products, 0, tile, jnp.where(keep, real, 0.0))
        put_split(products, 1, tile, jnp.where(keep, imag, 0.0))
    f_real, f_imag = split_sums(products, spread_pair)
    for tile in range(CHANNELS // 2):
        rows = slice(tile * MODES, (tile + 1) * MODES)
        where = slice(tile * 128, (tile + 1) * 128)
        weight_out[:, 0, where] = f_real[rows] * g_real + f_imag[rows] * g_imag
        weight_out[:, 1, where] = f_real[rows] * g_imag - f_imag[rows] * g_real


def sampled(waves, sampler, pair, lead):
    rows = rows_of(waves)
    mixed = jnp.dot(sampler, pair, preferred_element_type=f32)
    total = 0.0
    for slot, row in enumerate(rows):
        total = total + mixed[slot * 64 : (slot + 1) * 64] * lead[row : row + 1]
    return total


def fused_kernel(
    scale,
    tiles_ref,
    pos_ref,
    cot_hbm,
    feat_hbm,
    weight_hbm,
    weight_out,
    even_sampler,
    out_hbm,
    pair_hbm,
    lead_hbm,
    cot_ref,
    feat_ref,
    weight_ref,
    weight_tiles,
    pair_ref,
    lead_ref,
    rows_ref,
    acc,
    out_ref,
    part,
    from_mate,
    chip_sum,
    from_chip,
    products,
    own_block,
    grad_ref,
    odd_sampler,
    g_sum,
    load_sem,
    store_sem,
    mate_send,
    mate_recv,
    chip_send,
    chip_recv,
    grad_send,
    grad_recv,
    both_send,
    both_recv,
    from_level,
    level_sum,
    from_pencil,
    feat_send,
    feat_recv,
):
    slab = lax.axis_index("slab")
    pencil = lax.axis_index("pencil")
    core = slab % 2
    level = slab // 2
    parity = pencil // 8
    place = pencil % 8
    mate = (level * 2 + 1 - core, pencil)
    atoms = pos_ref.shape[1]
    own_rows = pl.ds(pl.multiple_of(place * MODES, MODES), MODES)

    load_cot = pltpu.make_async_copy(cot_hbm, cot_ref, load_sem.at[2])
    load_cot.start()
    load_feat = pltpu.make_async_copy(feat_hbm, feat_ref, load_sem.at[0])
    load_weight = pltpu.make_async_copy(weight_hbm, weight_ref, load_sem.at[1])
    load_feat.start()
    load_weight.start()

    def chip_peer(step):
        chip = (level * 16 + pencil + step + 1) % CHIPS
        return (chip // 16 * 2 + core, chip % 16)

    barrier = pltpu.get_barrier_semaphore()

    def greet(step, _):
        pl.semaphore_signal(barrier, inc=1, device_id=chip_peer(step), device_id_type=MESH_ID)
        return 0

    lax.fori_loop(0, CHIPS - 1, greet, 0)
    pl.semaphore_signal(barrier, inc=1, device_id=mate, device_id_type=MESH_ID)

    sub = 512
    chunk = 2048

    def phases(index):
        for piece in range(chunk // sub):
            start = index * chunk + piece * sub
            where = slice(start, start + sub)
            atom = start + lax.broadcasted_iota(jnp.int32, (1, sub), 1)
            live = jnp.where(atom < tiles_ref[0] * TILE, 1.0, 0.0).astype(f32)
            write_phases(pos_ref[:, where], live, lead_ref, pair_ref, where)

    def spread(values_ref, waves, base, where, add=False):
        rows = rows_of(waves)
        height = len(rows) * CHANNELS
        target = slice(base * CHANNELS, base * CHANNELS + height)
        values = values_ref[:, where].astype(f32)
        for slot, row in enumerate(rows):
            rows_ref[slot * 64 : slot * 64 + 64, where] = (
                values * lead_ref[row : row + 1, where]
            ).astype(bf16)
        product = lax.dot_general(
            pair_ref[:, where], rows_ref[0:height, where], last_last, preferred_element_type=f32
        )
        acc[:, target] = acc[:, target] + product if add else product

    def finish(kind, waves, base):
        sign = jnp.where(lax.broadcasted_iota(jnp.int32, (PAIRS, 128), 1) < CHANNELS, -1.0, 1.0)

        def put(index, block):
            part[kind, index // 4, index // 2 % 2, index % 2] = block.astype(bf16)

        for slot, wave in enumerate(waves):
            start = (base + 2 * slot) * CHANNELS
            if wave == 0:
                where = slice(start, start + CHANNELS)
                put(HALF, jnp.concatenate([acc[0:PAIRS, where], acc[PAIRS:, where]], 1))
                continue
            where = slice(start, start + 128)
            straight = acc[0:PAIRS, where]
            crossed = pltpu.roll(acc[PAIRS:, where], CHANNELS, 1)
            if wave < HALF:
                put(HALF + wave, straight + sign * crossed)
            put(HALF - wave, crossed - sign * straight)

    def mate_copy(kind, side):
        return pltpu.make_async_remote_copy(
            src_ref=part.at[kind, :, 1 - core, side],
            dst_ref=from_mate.at[kind, side],
            send_sem=mate_send.at[kind, side],
            recv_sem=mate_recv.at[kind, side],
            device_id=mate,
            device_id_type=MESH_ID,
        )

    def sum_chip(kind, side):
        mate_copy(kind, side).wait_recv()
        for height in range(4):
            total = part[kind, height, core, side].astype(f32) + from_mate[kind, side, height].astype(f32)
            chip_sum[kind, side, height] = total.astype(bf16)

    def to_owners(kind, side):
        sum_chip(kind, side)
        same = 1 - (parity + side) % 2

        def send(step, _):
            ahead = step + same
            target_level = (level + ahead // 8) % 4
            target_place = (place + ahead) % 8
            pltpu.make_async_remote_copy(
                src_ref=chip_sum.at[
                    kind, side, target_level, pl.ds(pl.multiple_of(target_place * MODES, MODES), MODES), :
                ],
                dst_ref=from_chip.at[kind, step + 31 - 31 * same],
                send_sem=chip_send.at[kind],
                recv_sem=chip_recv.at[kind],
                device_id=(target_level * 2 + core, side * 8 + target_place),
                device_id_type=MESH_ID,
            ).start()
            return 0

        lax.fori_loop(0, 32 - same, send, 0)

    def own_sum():
        every = from_chip.at[0]
        pltpu.make_async_copy(every, every, chip_recv.at[0]).wait()
        total = chip_sum[0, parity, level, own_rows, :].astype(f32)
        for source in range(CHIPS - 1):
            total = total + from_chip[0, source].astype(f32)
        return total * scale

    def features_to_levels():
        sum_chip(1, 1)
        sum_chip(1, 0)

        def send(step, _):
            target = (level + step) % 4
            pltpu.make_async_remote_copy(
                src_ref=chip_sum.at[1, :, target],
                dst_ref=from_level.at[3 - step],
                send_sem=feat_send.at[0],
                recv_sem=feat_recv.at[0],
                device_id=(target * 2 + core, pencil),
                device_id_type=MESH_ID,
            ).start()
            return 0

        lax.fori_loop(1, 4, send, 0)

    def features_to_pencils():
        pltpu.make_async_copy(from_level, from_level, feat_recv.at[0]).wait()
        for side in range(2):
            total = chip_sum[1, side, level].astype(f32)
            for source in range(3):
                total = total + from_level[source, side].astype(f32)
            level_sum[side] = total

        def send(step, _):
            target = (pencil + step) % 16
            pltpu.make_async_remote_copy(
                src_ref=level_sum.at[target // 8, pl.ds(pl.multiple_of(target % 8 * MODES, MODES), MODES), :],
                dst_ref=from_pencil.at[15 - step],
                send_sem=feat_send.at[1],
                recv_sem=feat_recv.at[1],
                device_id=(slab, target),
                device_id_type=MESH_ID,
            ).start()
            return 0

        lax.fori_loop(1, 16, send, 0)

    def feature_sum():
        pltpu.make_async_copy(from_pencil, from_pencil, feat_recv.at[1]).wait()
        total = level_sum[parity, own_rows, :]
        for source in range(15):
            total = total + from_pencil[source]
        return total * scale

    def lay_weights():
        load_weight.wait()
        for tile in range(CHANNELS // 2):
            for side in range(2):
                weight_tiles[side, tile] = weight_ref[:, side, tile * 128 : (tile + 1) * 128]

    def mix_and_share():
        total = own_sum()
        g_sum[...] = total
        g_real, g_imag = both_halves(total, False), both_halves(total, True)
        lanes = lax.broadcasted_iota(jnp.int32, (MODES, 128), 1)
        halves = jnp.where(
            lax.broadcasted_iota(jnp.int32, (128, 128), 0) // 64
            == lax.broadcasted_iota(jnp.int32, (128, 128), 1) % 2,
            1.0,
            0.0,
        ).astype(bf16)
        for tile in range(CHANNELS // 2):
            w_real = weight_tiles[0, tile]
            w_imag = weight_tiles[1, tile]
            put_split(products, 0, tile, w_real * g_real + w_imag * g_imag)
            put_split(products, 1, tile, w_real * g_imag - w_imag * g_real)
        real_sums, imag_sums = split_sums(products, halves)
        block = jnp.zeros((MODES, 128), f32)
        for tile in range(CHANNELS // 2):
            rows = slice(tile * MODES, (tile + 1) * MODES)
            mixed = jnp.where(lanes < 64, real_sums[rows], imag_sums[rows])
            block = block + jnp.where(lanes % 64 // 2 == tile, mixed, 0.0)
        own_block[...] = block.astype(bf16)
        grad_ref[parity, level, core, own_rows, :] = block.astype(bf16)

        def share(step, _):
            pltpu.make_async_remote_copy(
                src_ref=own_block,
                dst_ref=grad_ref.at[parity, level, core, own_rows, :],
                send_sem=grad_send,
                recv_sem=grad_recv.at[parity],
                device_id=chip_peer(step),
                device_id_type=MESH_ID,
            ).start()
            return 0

        lax.fori_loop(0, CHIPS - 1, share, 0)

    def both_copy(side):
        return pltpu.make_async_remote_copy(
            src_ref=grad_ref.at[side, :, core],
            dst_ref=grad_ref.at[side, :, core],
            send_sem=both_send.at[side],
            recv_sem=both_recv.at[side],
            device_id=mate,
            device_id_type=MESH_ID,
        )

    def forward(side):
        @pl.when(parity == side)
        def _():
            some = from_chip.at[0, pl.ds(0, 31)]
            pltpu.make_async_copy(some, some, grad_recv.at[side]).wait()

        @pl.when(parity != side)
        def _():
            some = from_chip.at[0, pl.ds(0, 32)]
            pltpu.make_async_copy(some, some, grad_recv.at[side]).wait()

        both_copy(side).start()

    def build_sampler(side, waves, sampler):
        blocks = flipped(grad_ref[side].reshape(8 * PAIRS, 128), identity_matrix())

        def block(index):
            return blocks[:, index // 2 * PAIRS : (index // 2 + 1) * PAIRS] * scale

        def put(slot, real, imag):
            sampler[slot * 64 : slot * 64 + 64, 0:PAIRS] = real.astype(bf16)
            sampler[slot * 64 : slot * 64 + 64, PAIRS:] = imag.astype(bf16)

        for slot, wave in enumerate(waves):
            minus = block(HALF - wave)
            if wave == 0:
                put(2 * slot, minus[0:64], minus[64:128])
                continue
            if wave < HALF:
                plus = block(HALF + wave)
                total, gap = plus + minus, plus - minus
            else:
                total, gap = minus, -minus
            put(2 * slot, total[0:64], total[64:128])
            put(2 * slot + 1, gap[64:128], -gap[0:64])

    width = 2048

    def store_out(index):
        where = pl.ds(pl.multiple_of(index * width, width), width)
        return pltpu.make_async_copy(out_ref.at[:, where], out_hbm.at[:, where], store_sem.at[index + 2])

    def sample(index):
        where = slice(index * width, (index + 1) * width)
        out_ref[:, where] = sampled(ODD, odd_sampler[...], pair_ref[:, where], lead_ref[:, where])
        store_out(index).start()

    phases(0)
    load_cot.wait()
    for index in range(atoms // chunk):
        if index + 1 < atoms // chunk:
            phases(index + 1)
        spread(cot_ref, ODD, 0, slice(index * chunk, (index + 1) * chunk), index > 0)
    finish(0, ODD, 0)
    pl.semaphore_wait(barrier, CHIPS)
    mate_copy(0, 1).start()
    store_pair = pltpu.make_async_copy(pair_ref, pair_hbm, store_sem.at[0])
    store_lead = pltpu.make_async_copy(lead_ref, lead_hbm, store_sem.at[1])
    store_pair.start()
    store_lead.start()
    whole = slice(0, atoms)
    low, high = EVEN[:2], EVEN[2:]
    spread(cot_ref, low, 8, whole)
    to_owners(0, 1)
    spread(cot_ref, high, 12, whole)
    finish(0, low, 8)
    finish(0, high, 12)
    mate_copy(0, 0).start()
    load_feat.wait()
    spread(feat_ref, ODD[:2], 0, whole)
    to_owners(0, 0)
    spread(feat_ref, ODD[2:], 4, whole)
    lay_weights()
    spread(feat_ref, low, 8, whole)

    @pl.when(parity == 1)
    def _():
        mix_and_share()

    spread(feat_ref, high, 12, whole)
    finish(1, ODD[:2], 0)
    finish(1, ODD[2:], 4)
    finish(1, low, 8)
    finish(1, high, 12)
    mate_copy(1, 1).start()
    mate_copy(1, 0).start()

    @pl.when(parity == 0)
    def _():
        mix_and_share()

    features_to_levels()
    forward(1)
    features_to_pencils()
    both_copy(1).wait_recv()
    build_sampler(1, ODD, odd_sampler)
    count = atoms // width
    for index in range(count // 2):
        sample(index)
    forward(0)
    for index in range(count // 2, count):
        sample(index)
    weight_gradient(g_sum[...], feature_sum(), weight_out, products)
    both_copy(0).wait_recv()
    build_sampler(0, EVEN, even_sampler)
    for kind in range(2):
        for side in range(2):
            mate_copy(kind, side).wait_send()
    every = from_chip.at[0]
    pltpu.make_async_copy(every, every, chip_send.at[0]).wait()
    pltpu.make_async_copy(from_level, from_level, feat_send.at[0]).wait()
    pltpu.make_async_copy(from_pencil, from_pencil, feat_send.at[1]).wait()
    pltpu.make_async_copy(every, every, grad_send).wait()
    both_copy(0).wait_send()
    both_copy(1).wait_send()
    store_pair.wait()
    store_lead.wait()
    for index in range(count):
        store_out(index).wait()


def fused_call(features, cotangent, positions, tiles, weight, scale):
    atoms = features.shape[1]
    vmem = pl.BlockSpec(memory_space=pltpu.VMEM)
    anywhere = pl.BlockSpec(memory_space=pl.ANY)
    return pl.pallas_call(
        functools.partial(fused_kernel, scale),
        out_shape=[
            jax.ShapeDtypeStruct(weight.shape, f32),
            jax.ShapeDtypeStruct((9 * CHANNELS, 2 * PAIRS), bf16),
            jax.ShapeDtypeStruct((CHANNELS, atoms), f32),
            jax.ShapeDtypeStruct((2 * PAIRS, atoms), bf16),
            jax.ShapeDtypeStruct((ROWS_L_PAD, atoms), f32),
        ],
        in_specs=[pl.BlockSpec(memory_space=pltpu.SMEM), vmem, anywhere, anywhere, anywhere],
        out_specs=[vmem, vmem, anywhere, anywhere, anywhere],
        scratch_shapes=[
            pltpu.VMEM((CHANNELS, atoms), bf16),
            pltpu.VMEM((CHANNELS, atoms), bf16),
            pltpu.VMEM(weight.shape, f32),
            pltpu.VMEM((2, CHANNELS // 2, MODES, 128), f32),
            pltpu.VMEM((2 * PAIRS, atoms), bf16),
            pltpu.VMEM((ROWS_L_PAD, atoms), f32),
            pltpu.VMEM((9 * CHANNELS, atoms), bf16),
            pltpu.VMEM((2 * PAIRS, (ROWS_L + 1) * CHANNELS), f32),
            pltpu.VMEM((CHANNELS, atoms), f32),
            pltpu.VMEM((2, 4, 2, 2, PAIRS, 128), bf16),
            pltpu.VMEM((2, 2, 4, PAIRS, 128), bf16),
            pltpu.VMEM((2, 2, 4, PAIRS, 128), bf16),
            pltpu.VMEM((1, CHIPS - 1, MODES, 128), bf16),
            pltpu.VMEM((4 * TILE_ROWS, 128), bf16),
            pltpu.VMEM((MODES, 128), bf16),
            pltpu.VMEM((2, 4, 2, PAIRS, 128), bf16),
            pltpu.VMEM((8 * CHANNELS, 2 * PAIRS), bf16),
            pltpu.VMEM((MODES, 128), f32),
            pltpu.SemaphoreType.DMA((3,)),
            pltpu.SemaphoreType.DMA((6,)),
            pltpu.SemaphoreType.DMA((2, 2)),
            pltpu.SemaphoreType.DMA((2, 2)),
            pltpu.SemaphoreType.DMA((2,)),
            pltpu.SemaphoreType.DMA((2,)),
            pltpu.SemaphoreType.DMA,
            pltpu.SemaphoreType.DMA((2,)),
            pltpu.SemaphoreType.DMA((2,)),
            pltpu.SemaphoreType.DMA((2,)),
            pltpu.VMEM((3, 2, PAIRS, 128), bf16),
            pltpu.VMEM((2, PAIRS, 128), f32),
            pltpu.VMEM((15, MODES, 128), f32),
            pltpu.SemaphoreType.DMA((2,)),
            pltpu.SemaphoreType.DMA((2,)),
        ],
        compiler_params=pltpu.CompilerParams(
            collective_id=0, has_side_effects=True, vmem_limit_bytes=VMEM_LIMIT
        ),
        name="fused",
    )(tiles, positions, cotangent, features, weight)


def last_kernel(
    weight_in, sampler_ref, pair_ref, lead_ref, part_ref, out_ref, weight_out, weight_ref, load_sem, store_sem
):
    step = pl.program_id(0)
    load = pltpu.make_async_copy(weight_in, weight_ref, load_sem)
    store = pltpu.make_async_copy(weight_ref, weight_out, store_sem)

    @pl.when(step == 0)
    def _():
        load.start()

    @pl.when(step == 1)
    def _():
        load.wait()
        store.start()

    out_ref[...] = part_ref[...] + sampled(EVEN, sampler_ref[...], pair_ref[...], lead_ref[...])

    @pl.when(step == pl.num_programs(0) - 1)
    def _():
        store.wait()


def last_call(weight_gradient_here, sampler, out, pair, lead):
    atoms = pair.shape[1]
    width = 2048
    return pl.pallas_call(
        last_kernel,
        grid=(atoms // width,),
        out_shape=[
            jax.ShapeDtypeStruct((CHANNELS, atoms), f32),
            jax.ShapeDtypeStruct(weight_gradient_here.shape, f32),
        ],
        in_specs=[
            pl.BlockSpec(memory_space=pl.ANY),
            pl.BlockSpec((9 * CHANNELS, 2 * PAIRS), lambda i: (0, 0)),
            pl.BlockSpec((2 * PAIRS, width), lambda i: (0, i)),
            pl.BlockSpec((ROWS_L_PAD, width), lambda i: (0, i)),
            pl.BlockSpec((CHANNELS, width), lambda i: (0, i)),
        ],
        out_specs=[
            pl.BlockSpec((CHANNELS, width), lambda i: (0, i)),
            pl.BlockSpec(memory_space=pl.ANY),
        ],
        scratch_shapes=[
            pltpu.VMEM(weight_gradient_here.shape, f32),
            pltpu.SemaphoreType.DMA,
            pltpu.SemaphoreType.DMA,
        ],
        compiler_params=pltpu.CompilerParams(vmem_limit_bytes=VMEM_LIMIT),
        name="last",
    )(weight_gradient_here, sampler, pair, lead, out)


def on_device(features, cotangent, positions, tiles, weight):
    devices_all = lax.axis_size("slab") * lax.axis_size("pencil")
    scale = 1.0 / math.sqrt(TILES_DEV * TILE * devices_all)
    fused = fused_call(features, cotangent, positions, tiles, weight, scale)
    return tuple(last_call(*fused))


def solution(mesh):
    return jax.shard_map(
        on_device,
        mesh=mesh,
        in_specs=(
            P(None, ("slab", "pencil")),
            P(None, ("slab", "pencil")),
            P(None, ("slab", "pencil")),
            P(("slab", "pencil")),
            P(("slab", "pencil"), None, None),
        ),
        out_specs=(P(None, ("slab", "pencil")), P(("slab", "pencil"), None, None)),
        check_vma=False,
    )
```

```python
import functools
import math

import jax
import jax.numpy as jnp
import numpy as np
from jax import lax
from jax.experimental import pallas as pl
from jax.experimental.pallas import tpu as pltpu
from jax.sharding import PartitionSpec as P

GRID = 256
KX = 16
KY = 16
KZ = 8
TILE = 128
TILES_DEV = 32
CHANNELS = 64
PAIRS = KY * KZ
HALF = KX // 2
ROWS_L = 2 * HALF + 1
ROWS_L_PAD = 24
STEP_FRACTION = 256
MODES = 16
CHIPS = 64
ODD, EVEN = (1, 3, 5, 7), (2, 4, 6, 8, 0)

bf16 = jnp.bfloat16
f32 = jnp.float32
last_last = (((1,), (1,)), ((), ()))
MESH_ID = pl.DeviceIdType.MESH
VMEM_LIMIT = 56 * 1024 * 1024


def spline_table(waves):
    basis = np.array(
        [[1, -3, 3, -1], [4, 0, -6, 3], [1, 3, 3, -3], [0, 0, 0, 1]], np.float64
    ) / 6.0
    turn = np.exp(-2j * np.pi * np.outer(waves, np.arange(4) - 1) / GRID)
    return turn @ basis


def column(values):
    rows = lax.broadcasted_iota(jnp.int32, (8, 1), 0)
    out = jnp.full((8, 1), float(values[0]), f32)
    for row in range(1, 8):
        out = jnp.where(rows == row, float(values[row]), out)
    return out


def axis_phase(position, first_wave):
    columns = position.shape[1]
    table = spline_table(np.arange(first_wave, first_wave + 8))
    wave = lax.broadcasted_iota(jnp.int32, (8, 1), 0) + first_wave
    cell = position >> 8
    fraction = (position & (STEP_FRACTION - 1)).astype(f32) * (1.0 / STEP_FRACTION)
    turns = ((wave * cell + GRID // 2) & (GRID - 1)) - GRID // 2
    half = turns.astype(f32) * (math.pi / GRID)
    square = half * half
    sine = -1.0 / 39916800.0
    for term in (1.0 / 362880.0, -1.0 / 5040.0, 1.0 / 120.0, -1.0 / 6.0, 1.0):
        sine = sine * square + term
    sine = sine * half
    cosine = 1.0 / 479001600.0
    for term in (-1.0 / 3628800.0, 1.0 / 40320.0, -1.0 / 720.0, 1.0 / 24.0, -0.5, 1.0):
        cosine = cosine * square + term
    turn_cos = 1.0 - 2.0 * sine * sine
    turn_sin = 2.0 * sine * cosine
    fraction = jnp.broadcast_to(fraction, (8, columns))
    stencil_real = column(table[:, 3].real)
    stencil_imag = column(table[:, 3].imag)
    for power in (2, 1, 0):
        stencil_real = stencil_real * fraction + column(table[:, power].real)
        stencil_imag = stencil_imag * fraction + column(table[:, power].imag)
    real = turn_cos * stencil_real + turn_sin * stencil_imag
    imag = turn_cos * stencil_imag - turn_sin * stencil_real
    return real, imag


def write_phases(position, live, lead_ref, pair_ref, where):
    lead_real, lead_imag = axis_phase(position[0:1], 1)
    side_real, side_imag = axis_phase(position[1:2], 1)
    depth_real, depth_imag = axis_phase(position[2:3], 0)
    lead_ref[0:8, where] = lead_real * live
    lead_ref[8:16, where] = lead_imag * live
    lead_ref[16:24, where] = jnp.broadcast_to(live, lead_real.shape)
    reals, imags = [None] * KY, [None] * KY
    reals[HALF], imags[HALF] = depth_real, depth_imag
    for wave in range(1, HALF + 1):
        real, imag = side_real[wave - 1 : wave], side_imag[wave - 1 : wave]
        rr, ii = real * depth_real, imag * depth_imag
        ri, ir = real * depth_imag, imag * depth_real
        if wave < HALF:
            reals[HALF + wave], imags[HALF + wave] = rr - ii, ri + ir
        reals[HALF - wave], imags[HALF - wave] = rr + ii, ri - ir
    for pair in range(HALF):
        rows = pl.ds(pair * 16, 16)
        pair_ref[rows, where] = jnp.concatenate(reals[2 * pair : 2 * pair + 2], 0).astype(bf16)
        rows = pl.ds(PAIRS + pair * 16, 16)
        pair_ref[rows, where] = jnp.concatenate(imags[2 * pair : 2 * pair + 2], 0).astype(bf16)


def identity_matrix():
    rows = lax.broadcasted_iota(jnp.int32, (128, 128), 0)
    columns = lax.broadcasted_iota(jnp.int32, (128, 128), 1)
    return jnp.where(rows == columns, 1.0, 0.0).astype(bf16)


def flipped(matrix, eye):
    return lax.dot_general(eye, matrix, last_last, preferred_element_type=f32)


TILE_ROWS = CHANNELS // 2 * MODES


def put_split(products, side, tile, values):
    high = values.astype(bf16)
    rows = pl.ds((2 * side * CHANNELS // 2 + tile) * MODES, MODES)
    products[rows, :] = high
    rows = pl.ds(((2 * side + 1) * CHANNELS // 2 + tile) * MODES, MODES)
    products[rows, :] = (values - high.astype(f32)).astype(bf16)


def split_sums(products, matrix):
    every = jnp.dot(products[...], matrix, preferred_element_type=f32)
    parts = [every[index * TILE_ROWS : (index + 1) * TILE_ROWS] for index in range(4)]
    return parts[0] + parts[1], parts[2] + parts[3]


def split_product(values, matrix):
    high = values.astype(bf16)
    low = (values - high.astype(f32)).astype(bf16)
    return jnp.dot(high, matrix, preferred_element_type=f32) + jnp.dot(
        low, matrix, preferred_element_type=f32
    )


def both_halves(values, upper):
    part = values[:, 64:128] if upper else values[:, 0:64]
    return jnp.concatenate([part, part], 1)


def rows_of(waves):
    rows = []
    for wave in waves:
        rows += [wave - 1, HALF + wave - 1] if wave else [2 * HALF]
    return rows


def fused_kernel(
    scale,
    tiles_ref,
    pos_ref,
    cot_ref,
    feat_hbm,
    weight_hbm,
    out_ref,
    spectrum_ref,
    feat_ref,
    weight_ref,
    weight_tiles,
    pair_ref,
    lead_ref,
    rows_ref,
    acc,
    part,
    from_mate,
    chip_sum,
    from_chip,
    products,
    own_block,
    grad_ref,
    sampler,
    load_sem,
    mate_send,
    mate_recv,
    chip_send,
    chip_recv,
    grad_send,
    grad_recv,
    both_send,
    both_recv,
):
    slab = lax.axis_index("slab")
    pencil = lax.axis_index("pencil")
    core = slab % 2
    level = slab // 2
    parity = pencil // 8
    place = pencil % 8
    mate = (level * 2 + 1 - core, pencil)
    atoms = pos_ref.shape[1]
    own_rows = pl.ds(pl.multiple_of(place * MODES, MODES), MODES)

    load_feat = pltpu.make_async_copy(feat_hbm, feat_ref, load_sem.at[0])
    load_weight = pltpu.make_async_copy(weight_hbm, weight_ref, load_sem.at[1])
    load_feat.start()
    load_weight.start()

    def chip_peer(step):
        chip = (level * 16 + pencil + step) % CHIPS
        return (chip // 16 * 2 + core, chip % 16)

    barrier = pltpu.get_barrier_semaphore()

    def greet(step, _):
        pl.semaphore_signal(barrier, inc=1, device_id=chip_peer(step), device_id_type=MESH_ID)
        return 0

    lax.fori_loop(1, CHIPS, greet, 0)
    pl.semaphore_signal(barrier, inc=1, device_id=mate, device_id_type=MESH_ID)

    sub = 512

    def phases(piece, _):
        where = pl.ds(pl.multiple_of(piece * sub, sub), sub)
        index = piece * sub + lax.broadcasted_iota(jnp.int32, (1, sub), 1)
        live = jnp.where(index < tiles_ref[0] * TILE, 1.0, 0.0).astype(f32)
        write_phases(pos_ref[:, where], live, lead_ref, pair_ref, where)
        return 0

    lax.fori_loop(0, atoms // sub, phases, 0)

    chunk = 2048

    def spread(values_ref, waves, base, first, last):
        rows = rows_of(waves)
        height = len(rows) * CHANNELS
        target = slice(base * CHANNELS, base * CHANNELS + height)

        def one(index, _):
            where = pl.ds(pl.multiple_of(index * chunk, chunk), chunk)
            values = values_ref[:, where].astype(f32)
            for place_of, row in enumerate(rows):
                rows_ref[place_of * 64 : place_of * 64 + 64, :] = (
                    values * lead_ref[row : row + 1, where]
                ).astype(bf16)
            acc[:, target] += lax.dot_general(
                pair_ref[:, where], rows_ref[0:height, :], last_last, preferred_element_type=f32
            )
            return 0

        if first == 0:
            acc[:, target] = jnp.zeros((2 * PAIRS, height), f32)
        lax.fori_loop(first, last, one, 0)

    def finish(kind, waves, base):
        sign = jnp.where(lax.broadcasted_iota(jnp.int32, (PAIRS, 128), 1) < CHANNELS, -1.0, 1.0)

        def put(index, block):
            part[kind, index // 4, index // 2 % 2, index % 2] = block.astype(bf16)

        for slot, wave in enumerate(waves):
            start = (base + 2 * slot) * CHANNELS
            if wave == 0:
                where = slice(start, start + CHANNELS)
                put(HALF, jnp.concatenate([acc[0:PAIRS, where], acc[PAIRS:, where]], 1))
                continue
            where = slice(start, start + 128)
            straight = acc[0:PAIRS, where]
            crossed = pltpu.roll(acc[PAIRS:, where], CHANNELS, 1)
            if wave < HALF:
                put(HALF + wave, straight + sign * crossed)
            put(HALF - wave, crossed - sign * straight)

    def mate_copy(kind, side):
        return pltpu.make_async_remote_copy(
            src_ref=part.at[kind, :, 1 - core, side],
            dst_ref=from_mate.at[kind, side],
            send_sem=mate_send.at[kind, side],
            recv_sem=mate_recv.at[kind, side],
            device_id=mate,
            device_id_type=MESH_ID,
        )

    def to_owners(kind, side):
        mate_copy(kind, side).wait_recv()
        for height in range(4):
            total = part[kind, height, core, side].astype(f32) + from_mate[kind, side, height].astype(f32)
            chip_sum[kind, side, height] = total.astype(bf16)
        same = 1 - (parity + side) % 2

        def send(step, _):
            target_level = (level + step // 8) % 4
            target_place = (place + step) % 8
            pltpu.make_async_remote_copy(
                src_ref=chip_sum.at[
                    kind, side, target_level, pl.ds(pl.multiple_of(target_place * MODES, MODES), MODES), :
                ],
                dst_ref=from_chip.at[kind, step + 31 - 32 * same],
                send_sem=chip_send.at[kind],
                recv_sem=chip_recv.at[kind],
                device_id=(target_level * 2 + core, side * 8 + target_place),
                device_id_type=MESH_ID,
            ).start()
            return 0

        lax.fori_loop(same, 32, send, 0)

    def own_sum(kind):
        every = from_chip.at[kind]
        pltpu.make_async_copy(every, every, chip_recv.at[kind]).wait()
        total = chip_sum[kind, parity, level, own_rows, :].astype(f32)
        for source in range(CHIPS - 1):
            total = total + from_chip[kind, source].astype(f32)
        total = total * scale
        spectrum_ref[kind] = total
        return total

    def lay_weights():
        load_weight.wait()
        for tile in range(CHANNELS // 2):
            for side in range(2):
                weight_tiles[side, tile] = weight_ref[:, side, tile * 128 : (tile + 1) * 128]

    def mix_and_share():
        total = own_sum(0)
        g_real, g_imag = both_halves(total, False), both_halves(total, True)
        lanes = lax.broadcasted_iota(jnp.int32, (MODES, 128), 1)
        halves = jnp.where(
            lax.broadcasted_iota(jnp.int32, (128, 128), 0) // 64
            == lax.broadcasted_iota(jnp.int32, (128, 128), 1) % 2,
            1.0,
            0.0,
        ).astype(bf16)
        for tile in range(CHANNELS // 2):
            w_real = weight_tiles[0, tile]
            w_imag = weight_tiles[1, tile]
            put_split(products, 0, tile, w_real * g_real + w_imag * g_imag)
            put_split(products, 1, tile, w_real * g_imag - w_imag * g_real)
        real_sums, imag_sums = split_sums(products, halves)
        block = jnp.zeros((MODES, 128), f32)
        for tile in range(CHANNELS // 2):
            rows = slice(tile * MODES, (tile + 1) * MODES)
            mixed = jnp.where(lanes < 64, real_sums[rows], imag_sums[rows])
            block = block + jnp.where(lanes % 64 // 2 == tile, mixed, 0.0)
        own_block[...] = block.astype(bf16)
        grad_ref[parity, level, core, own_rows, :] = block.astype(bf16)

        def share(step, _):
            pltpu.make_async_remote_copy(
                src_ref=own_block,
                dst_ref=grad_ref.at[parity, level, core, own_rows, :],
                send_sem=grad_send,
                recv_sem=grad_recv.at[parity],
                device_id=chip_peer(step),
                device_id_type=MESH_ID,
            ).start()
            return 0

        lax.fori_loop(1, CHIPS, share, 0)

    def both_copy(side):
        return pltpu.make_async_remote_copy(
            src_ref=grad_ref.at[side, :, core],
            dst_ref=grad_ref.at[side, :, core],
            send_sem=both_send.at[side],
            recv_sem=both_recv.at[side],
            device_id=mate,
            device_id_type=MESH_ID,
        )

    def forward(side):
        @pl.when(parity == side)
        def _():
            some = from_chip.at[0, pl.ds(0, 31)]
            pltpu.make_async_copy(some, some, grad_recv.at[side]).wait()

        @pl.when(parity != side)
        def _():
            some = from_chip.at[0, pl.ds(0, 32)]
            pltpu.make_async_copy(some, some, grad_recv.at[side]).wait()

        both_copy(side).start()

    def build_sampler(side, waves):
        blocks = flipped(grad_ref[side].reshape(8 * PAIRS, 128), identity_matrix())

        def block(index):
            return blocks[:, index // 2 * PAIRS : (index // 2 + 1) * PAIRS] * scale

        def put(slot, real, imag):
            sampler[slot * 64 : slot * 64 + 64, 0:PAIRS] = real.astype(bf16)
            sampler[slot * 64 : slot * 64 + 64, PAIRS:] = imag.astype(bf16)

        for slot, wave in enumerate(waves):
            minus = block(HALF - wave)
            if wave == 0:
                put(2 * slot, minus[0:64], minus[64:128])
                continue
            if wave < HALF:
                plus = block(HALF + wave)
                total, gap = plus + minus, plus - minus
            else:
                total, gap = minus, -minus
            put(2 * slot, total[0:64], total[64:128])
            put(2 * slot + 1, gap[64:128], -gap[0:64])

    width = 2048

    def sample(waves, add, first, last):
        rows = rows_of(waves)

        def one(index, _):
            where = pl.ds(pl.multiple_of(index * width, width), width)
            mixed = jnp.dot(
                sampler[0 : len(rows) * 64, :], pair_ref[:, where], preferred_element_type=f32
            )
            total = out_ref[:, where] if add else 0.0
            for slot, row in enumerate(rows):
                total = total + mixed[slot * 64 : (slot + 1) * 64] * lead_ref[row : row + 1, where]
            out_ref[:, where] = total
            return 0

        lax.fori_loop(first, last, one, 0)

    steps = atoms // chunk
    spread(cot_ref, ODD, 0, 0, steps)
    finish(0, ODD, 0)
    pl.semaphore_wait(barrier, CHIPS)
    mate_copy(0, 1).start()
    spread(cot_ref, EVEN, 8, 0, steps)
    finish(0, EVEN, 8)
    mate_copy(0, 0).start()
    to_owners(0, 1)
    load_feat.wait()
    every_wave = ODD + EVEN
    spread(feat_ref, every_wave, 0, 0, 1)
    to_owners(0, 0)
    spread(feat_ref, every_wave, 0, 1, 2)
    lay_weights()
    spread(feat_ref, every_wave, 0, 2, 3)

    @pl.when(parity == 1)
    def _():
        mix_and_share()

    spread(feat_ref, every_wave, 0, 3, steps)

    @pl.when(parity == 0)
    def _():
        mix_and_share()

    finish(1, every_wave, 0)
    mate_copy(1, 1).start()
    mate_copy(1, 0).start()
    forward(1)
    to_owners(1, 1)
    to_owners(1, 0)
    both_copy(1).wait_recv()
    build_sampler(1, ODD)
    half = atoms // width // 2
    sample(ODD, False, 0, half)
    forward(0)
    sample(ODD, False, half, 2 * half)
    both_copy(0).wait_recv()
    build_sampler(0, EVEN)
    sample(EVEN, True, 0, 2 * half)
    own_sum(1)
    for kind in range(2):
        for side in range(2):
            mate_copy(kind, side).wait_send()
        every = from_chip.at[kind]
        pltpu.make_async_copy(every, every, chip_send.at[kind]).wait()
    every = from_chip.at[0]
    pltpu.make_async_copy(every, every, grad_send).wait()
    both_copy(0).wait_send()
    both_copy(1).wait_send()


def fused_call(features, cotangent, positions, tiles, weight, scale):
    atoms = features.shape[1]
    vmem = pl.BlockSpec(memory_space=pltpu.VMEM)
    anywhere = pl.BlockSpec(memory_space=pl.ANY)
    return pl.pallas_call(
        functools.partial(fused_kernel, scale),
        out_shape=[
            jax.ShapeDtypeStruct((CHANNELS, atoms), f32),
            jax.ShapeDtypeStruct((2, MODES, 128), f32),
        ],
        in_specs=[pl.BlockSpec(memory_space=pltpu.SMEM), vmem, vmem, anywhere, anywhere],
        out_specs=[vmem, vmem],
        scratch_shapes=[
            pltpu.VMEM((CHANNELS, atoms), bf16),
            pltpu.VMEM(weight.shape, f32),
            pltpu.VMEM((2, CHANNELS // 2, MODES, 128), f32),
            pltpu.VMEM((2 * PAIRS, atoms), bf16),
            pltpu.VMEM((ROWS_L_PAD, atoms), f32),
            pltpu.VMEM((ROWS_L * CHANNELS, 2048), bf16),
            pltpu.VMEM((2 * PAIRS, (ROWS_L + 1) * CHANNELS), f32),
            pltpu.VMEM((2, 4, 2, 2, PAIRS, 128), bf16),
            pltpu.VMEM((2, 2, 4, PAIRS, 128), bf16),
            pltpu.VMEM((2, 2, 4, PAIRS, 128), bf16),
            pltpu.VMEM((2, CHIPS - 1, MODES, 128), bf16),
            pltpu.VMEM((4 * TILE_ROWS, 128), bf16),
            pltpu.VMEM((MODES, 128), bf16),
            pltpu.VMEM((2, 4, 2, PAIRS, 128), bf16),
            pltpu.VMEM((9 * CHANNELS, 2 * PAIRS), bf16),
            pltpu.SemaphoreType.DMA((2,)),
            pltpu.SemaphoreType.DMA((2, 2)),
            pltpu.SemaphoreType.DMA((2, 2)),
            pltpu.SemaphoreType.DMA((2,)),
            pltpu.SemaphoreType.DMA((2,)),
            pltpu.SemaphoreType.DMA,
            pltpu.SemaphoreType.DMA((2,)),
            pltpu.SemaphoreType.DMA((2,)),
            pltpu.SemaphoreType.DMA((2,)),
        ],
        compiler_params=pltpu.CompilerParams(
            collective_id=0, has_side_effects=True, vmem_limit_bytes=VMEM_LIMIT
        ),
        name="fused",
    )(tiles, positions, cotangent, features, weight)


def weight_kernel(spectrum_ref, out_ref, columns):
    lanes = lax.broadcasted_iota(jnp.int32, (MODES, 128), 1)
    spread_pair = jnp.where(
        lax.broadcasted_iota(jnp.int32, (128, 128), 0) % 2
        == lax.broadcasted_iota(jnp.int32, (128, 128), 1) // 64,
        1.0,
        0.0,
    ).astype(bf16)
    g_real, g_imag = both_halves(spectrum_ref[0], False), both_halves(spectrum_ref[0], True)
    real, imag = both_halves(spectrum_ref[1], False), both_halves(spectrum_ref[1], True)
    for tile in range(CHANNELS // 2):
        keep = lanes // 2 == tile
        columns[0, tile * MODES : (tile + 1) * MODES] = jnp.where(keep, real, 0.0)
        columns[1, tile * MODES : (tile + 1) * MODES] = jnp.where(keep, imag, 0.0)
    f_real = split_product(columns[0], spread_pair)
    f_imag = split_product(columns[1], spread_pair)
    for tile in range(CHANNELS // 2):
        rows = slice(tile * MODES, (tile + 1) * MODES)
        where = slice(tile * 128, (tile + 1) * 128)
        out_ref[:, 0, where] = f_real[rows] * g_real + f_imag[rows] * g_imag
        out_ref[:, 1, where] = f_real[rows] * g_imag - f_imag[rows] * g_real


def weight_call(spectrum):
    vmem = pl.BlockSpec(memory_space=pltpu.VMEM)
    return pl.pallas_call(
        weight_kernel,
        out_shape=jax.ShapeDtypeStruct((MODES, 2, CHANNELS * CHANNELS), f32),
        in_specs=[vmem],
        out_specs=vmem,
        scratch_shapes=[pltpu.VMEM((2, CHANNELS // 2 * MODES, 128), f32)],
        compiler_params=pltpu.CompilerParams(vmem_limit_bytes=16 * 1024 * 1024),
        name="weight_gradient",
    )(spectrum)


def on_device(features, cotangent, positions, tiles, weight):
    devices_all = lax.axis_size("slab") * lax.axis_size("pencil")
    scale = 1.0 / math.sqrt(TILES_DEV * TILE * devices_all)
    gradient, spectrum = fused_call(features, cotangent, positions, tiles, weight, scale)
    return gradient, weight_call(spectrum)


def solution(mesh):
    return jax.shard_map(
        on_device,
        mesh=mesh,
        in_specs=(
            P(None, ("slab", "pencil")),
            P(None, ("slab", "pencil")),
            P(None, ("slab", "pencil")),
            P(("slab", "pencil")),
            P(("slab", "pencil"), None, None),
        ),
        out_specs=(P(None, ("slab", "pencil")), P(("slab", "pencil"), None, None)),
        check_vma=False,
    )
```

```python
import functools
import math

import jax
import jax.numpy as jnp
import numpy as np
from jax import lax
from jax.experimental import pallas as pl
from jax.experimental.pallas import tpu as pltpu
from jax.sharding import PartitionSpec as P

GRID = 256
KX = 16
KY = 16
KZ = 8
TILE = 128
TILES_DEV = 32
CHANNELS = 64
PAIRS = KY * KZ
HALF = KX // 2
ROWS_L = 2 * HALF + 1
ROWS_L_PAD = 24
STEP_FRACTION = 256
MODES = 16
CHIPS = 64
ODD, EVEN = (1, 3, 5, 7), (2, 4, 6, 8, 0)

bf16 = jnp.bfloat16
f32 = jnp.float32
last_last = (((1,), (1,)), ((), ()))
MESH_ID = pl.DeviceIdType.MESH
VMEM_LIMIT = 56 * 1024 * 1024


def spline_table(waves):
    basis = np.array(
        [[1, -3, 3, -1], [4, 0, -6, 3], [1, 3, 3, -3], [0, 0, 0, 1]], np.float64
    ) / 6.0
    turn = np.exp(-2j * np.pi * np.outer(waves, np.arange(4) - 1) / GRID)
    return turn @ basis


def column(values):
    rows = lax.broadcasted_iota(jnp.int32, (8, 1), 0)
    out = jnp.full((8, 1), float(values[0]), f32)
    for row in range(1, 8):
        out = jnp.where(rows == row, float(values[row]), out)
    return out


def axis_phase(position, first_wave):
    columns = position.shape[1]
    table = spline_table(np.arange(first_wave, first_wave + 8))
    wave = lax.broadcasted_iota(jnp.int32, (8, 1), 0) + first_wave
    cell = position >> 8
    fraction = (position & (STEP_FRACTION - 1)).astype(f32) * (1.0 / STEP_FRACTION)
    turns = ((wave * cell + GRID // 2) & (GRID - 1)) - GRID // 2
    half = turns.astype(f32) * (math.pi / GRID)
    square = half * half
    sine = -1.0 / 39916800.0
    for term in (1.0 / 362880.0, -1.0 / 5040.0, 1.0 / 120.0, -1.0 / 6.0, 1.0):
        sine = sine * square + term
    sine = sine * half
    cosine = 1.0 / 479001600.0
    for term in (-1.0 / 3628800.0, 1.0 / 40320.0, -1.0 / 720.0, 1.0 / 24.0, -0.5, 1.0):
        cosine = cosine * square + term
    turn_cos = 1.0 - 2.0 * sine * sine
    turn_sin = 2.0 * sine * cosine
    fraction = jnp.broadcast_to(fraction, (8, columns))
    stencil_real = column(table[:, 3].real)
    stencil_imag = column(table[:, 3].imag)
    for power in (2, 1, 0):
        stencil_real = stencil_real * fraction + column(table[:, power].real)
        stencil_imag = stencil_imag * fraction + column(table[:, power].imag)
    real = turn_cos * stencil_real + turn_sin * stencil_imag
    imag = turn_cos * stencil_imag - turn_sin * stencil_real
    return real, imag


def write_phases(position, live, lead_ref, pair_ref, where):
    lead_real, lead_imag = axis_phase(position[0:1], 1)
    side_real, side_imag = axis_phase(position[1:2], 1)
    depth_real, depth_imag = axis_phase(position[2:3], 0)
    lead_ref[0:8, where] = lead_real * live
    lead_ref[8:16, where] = lead_imag * live
    lead_ref[16:24, where] = jnp.broadcast_to(live, lead_real.shape)
    reals, imags = [None] * KY, [None] * KY
    reals[HALF], imags[HALF] = depth_real, depth_imag
    for wave in range(1, HALF + 1):
        real, imag = side_real[wave - 1 : wave], side_imag[wave - 1 : wave]
        rr, ii = real * depth_real, imag * depth_imag
        ri, ir = real * depth_imag, imag * depth_real
        if wave < HALF:
            reals[HALF + wave], imags[HALF + wave] = rr - ii, ri + ir
        reals[HALF - wave], imags[HALF - wave] = rr + ii, ri - ir
    for pair in range(HALF):
        rows = pl.ds(pair * 16, 16)
        pair_ref[rows, where] = jnp.concatenate(reals[2 * pair : 2 * pair + 2], 0).astype(bf16)
        rows = pl.ds(PAIRS + pair * 16, 16)
        pair_ref[rows, where] = jnp.concatenate(imags[2 * pair : 2 * pair + 2], 0).astype(bf16)


def identity_matrix():
    rows = lax.broadcasted_iota(jnp.int32, (128, 128), 0)
    columns = lax.broadcasted_iota(jnp.int32, (128, 128), 1)
    return jnp.where(rows == columns, 1.0, 0.0).astype(bf16)


def flipped(matrix, eye):
    return lax.dot_general(eye, matrix, last_last, preferred_element_type=f32)


TILE_ROWS = CHANNELS // 2 * MODES


def put_split(products, side, tile, values):
    high = values.astype(bf16)
    rows = pl.ds((2 * side * CHANNELS // 2 + tile) * MODES, MODES)
    products[rows, :] = high
    rows = pl.ds(((2 * side + 1) * CHANNELS // 2 + tile) * MODES, MODES)
    products[rows, :] = (values - high.astype(f32)).astype(bf16)


def split_sums(products, matrix):
    every = jnp.dot(products[...], matrix, preferred_element_type=f32)
    parts = [every[index * TILE_ROWS : (index + 1) * TILE_ROWS] for index in range(4)]
    return parts[0] + parts[1], parts[2] + parts[3]


def split_product(values, matrix):
    high = values.astype(bf16)
    low = (values - high.astype(f32)).astype(bf16)
    return jnp.dot(high, matrix, preferred_element_type=f32) + jnp.dot(
        low, matrix, preferred_element_type=f32
    )


def both_halves(values, upper):
    part = values[:, 64:128] if upper else values[:, 0:64]
    return jnp.concatenate([part, part], 1)


def rows_of(waves):
    rows = []
    for wave in waves:
        rows += [wave - 1, HALF + wave - 1] if wave else [2 * HALF]
    return rows


def fused_kernel(
    scale,
    tiles_ref,
    pos_ref,
    cot_ref,
    feat_hbm,
    weight_hbm,
    out_ref,
    spectrum_ref,
    feat_ref,
    weight_ref,
    weight_tiles,
    pair_ref,
    lead_ref,
    rows_ref,
    acc,
    part,
    from_mate,
    chip_sum,
    from_chip,
    products,
    own_block,
    grad_ref,
    sampler,
    load_sem,
    mate_send,
    mate_recv,
    chip_send,
    chip_recv,
    grad_send,
    grad_recv,
    both_send,
    both_recv,
):
    slab = lax.axis_index("slab")
    pencil = lax.axis_index("pencil")
    core = slab % 2
    level = slab // 2
    parity = pencil // 8
    place = pencil % 8
    mate = (level * 2 + 1 - core, pencil)
    atoms = pos_ref.shape[1]
    own_rows = pl.ds(pl.multiple_of(place * MODES, MODES), MODES)

    load_feat = pltpu.make_async_copy(feat_hbm, feat_ref, load_sem.at[0])
    load_weight = pltpu.make_async_copy(weight_hbm, weight_ref, load_sem.at[1])
    load_feat.start()
    load_weight.start()

    def chip_peer(step):
        chip = (level * 16 + pencil + step) % CHIPS
        return (chip // 16 * 2 + core, chip % 16)

    barrier = pltpu.get_barrier_semaphore()

    def greet(step, _):
        pl.semaphore_signal(barrier, inc=1, device_id=chip_peer(step), device_id_type=MESH_ID)
        return 0

    lax.fori_loop(1, CHIPS, greet, 0)
    pl.semaphore_signal(barrier, inc=1, device_id=mate, device_id_type=MESH_ID)

    sub = 512

    def phases(piece, _):
        where = pl.ds(pl.multiple_of(piece * sub, sub), sub)
        index = piece * sub + lax.broadcasted_iota(jnp.int32, (1, sub), 1)
        live = jnp.where(index < tiles_ref[0] * TILE, 1.0, 0.0).astype(f32)
        write_phases(pos_ref[:, where], live, lead_ref, pair_ref, where)
        return 0

    lax.fori_loop(0, atoms // sub, phases, 0)

    chunk = 2048

    def spread(values_ref, waves, base, first, last):
        rows = rows_of(waves)
        height = len(rows) * CHANNELS
        target = slice(base * CHANNELS, base * CHANNELS + height)

        def one(index, _):
            where = pl.ds(pl.multiple_of(index * chunk, chunk), chunk)
            values = values_ref[:, where].astype(f32)
            for place_of, row in enumerate(rows):
                rows_ref[place_of * 64 : place_of * 64 + 64, :] = (
                    values * lead_ref[row : row + 1, where]
                ).astype(bf16)
            acc[:, target] += lax.dot_general(
                pair_ref[:, where], rows_ref[0:height, :], last_last, preferred_element_type=f32
            )
            return 0

        if first == 0:
            acc[:, target] = jnp.zeros((2 * PAIRS, height), f32)
        lax.fori_loop(first, last, one, 0)

    def finish(kind, waves, base):
        sign = jnp.where(lax.broadcasted_iota(jnp.int32, (PAIRS, 128), 1) < CHANNELS, -1.0, 1.0)

        def put(index, block):
            part[kind, index // 4, index // 2 % 2, index % 2] = block.astype(bf16)

        for slot, wave in enumerate(waves):
            start = (base + 2 * slot) * CHANNELS
            if wave == 0:
                where = slice(start, start + CHANNELS)
                put(HALF, jnp.concatenate([acc[0:PAIRS, where], acc[PAIRS:, where]], 1))
                continue
            where = slice(start, start + 128)
            straight = acc[0:PAIRS, where]
            crossed = pltpu.roll(acc[PAIRS:, where], CHANNELS, 1)
            if wave < HALF:
                put(HALF + wave, straight + sign * crossed)
            put(HALF - wave, crossed - sign * straight)

    def mate_copy(kind, side):
        return pltpu.make_async_remote_copy(
            src_ref=part.at[kind, :, 1 - core, side],
            dst_ref=from_mate.at[kind, side],
            send_sem=mate_send.at[kind, side],
            recv_sem=mate_recv.at[kind, side],
            device_id=mate,
            device_id_type=MESH_ID,
        )

    def to_owners(kind, side):
        mate_copy(kind, side).wait_recv()
        for height in range(4):
            total = part[kind, height, core, side].astype(f32) + from_mate[kind, side, height].astype(f32)
            chip_sum[kind, side, height] = total.astype(bf16)
        same = 1 - (parity + side) % 2

        def send(step, _):
            target_level = (level + step // 8) % 4
            target_place = (place + step) % 8
            pltpu.make_async_remote_copy(
                src_ref=chip_sum.at[
                    kind, side, target_level, pl.ds(pl.multiple_of(target_place * MODES, MODES), MODES), :
                ],
                dst_ref=from_chip.at[kind, step + 31 - 32 * same],
                send_sem=chip_send.at[kind],
                recv_sem=chip_recv.at[kind],
                device_id=(target_level * 2 + core, side * 8 + target_place),
                device_id_type=MESH_ID,
            ).start()
            return 0

        lax.fori_loop(same, 32, send, 0)

    def own_sum(kind):
        every = from_chip.at[kind]
        pltpu.make_async_copy(every, every, chip_recv.at[kind]).wait()
        total = chip_sum[kind, parity, level, own_rows, :].astype(f32)
        for source in range(CHIPS - 1):
            total = total + from_chip[kind, source].astype(f32)
        total = total * scale
        spectrum_ref[kind] = total
        return total

    def lay_weights():
        load_weight.wait()
        for tile in range(CHANNELS // 2):
            for side in range(2):
                weight_tiles[side, tile] = weight_ref[:, side, tile * 128 : (tile + 1) * 128]

    def mix_and_share():
        total = own_sum(0)
        g_real, g_imag = both_halves(total, False), both_halves(total, True)
        lanes = lax.broadcasted_iota(jnp.int32, (MODES, 128), 1)
        halves = jnp.where(
            lax.broadcasted_iota(jnp.int32, (128, 128), 0) // 64
            == lax.broadcasted_iota(jnp.int32, (128, 128), 1) % 2,
            1.0,
            0.0,
        ).astype(bf16)
        for tile in range(CHANNELS // 2):
            w_real = weight_tiles[0, tile]
            w_imag = weight_tiles[1, tile]
            put_split(products, 0, tile, w_real * g_real + w_imag * g_imag)
            put_split(products, 1, tile, w_real * g_imag - w_imag * g_real)
        real_sums, imag_sums = split_sums(products, halves)
        block = jnp.zeros((MODES, 128), f32)
        for tile in range(CHANNELS // 2):
            rows = slice(tile * MODES, (tile + 1) * MODES)
            mixed = jnp.where(lanes < 64, real_sums[rows], imag_sums[rows])
            block = block + jnp.where(lanes % 64 // 2 == tile, mixed, 0.0)
        own_block[...] = block.astype(bf16)
        grad_ref[parity, level, core, own_rows, :] = block.astype(bf16)

        def share(step, _):
            pltpu.make_async_remote_copy(
                src_ref=own_block,
                dst_ref=grad_ref.at[parity, level, core, own_rows, :],
                send_sem=grad_send,
                recv_sem=grad_recv.at[parity],
                device_id=chip_peer(step),
                device_id_type=MESH_ID,
            ).start()
            return 0

        lax.fori_loop(1, CHIPS, share, 0)

    def both_copy(side):
        return pltpu.make_async_remote_copy(
            src_ref=grad_ref.at[side, :, core],
            dst_ref=grad_ref.at[side, :, core],
            send_sem=both_send.at[side],
            recv_sem=both_recv.at[side],
            device_id=mate,
            device_id_type=MESH_ID,
        )

    def forward(side):
        @pl.when(parity == side)
        def _():
            some = from_chip.at[0, pl.ds(0, 31)]
            pltpu.make_async_copy(some, some, grad_recv.at[side]).wait()

        @pl.when(parity != side)
        def _():
            some = from_chip.at[0, pl.ds(0, 32)]
            pltpu.make_async_copy(some, some, grad_recv.at[side]).wait()

        both_copy(side).start()

    def build_sampler(side, waves):
        blocks = flipped(grad_ref[side].reshape(8 * PAIRS, 128), identity_matrix())

        def block(index):
            return blocks[:, index // 2 * PAIRS : (index // 2 + 1) * PAIRS] * scale

        def put(slot, real, imag):
            sampler[slot * 64 : slot * 64 + 64, 0:PAIRS] = real.astype(bf16)
            sampler[slot * 64 : slot * 64 + 64, PAIRS:] = imag.astype(bf16)

        for slot, wave in enumerate(waves):
            minus = block(HALF - wave)
            if wave == 0:
                put(2 * slot, minus[0:64], minus[64:128])
                continue
            if wave < HALF:
                plus = block(HALF + wave)
                total, gap = plus + minus, plus - minus
            else:
                total, gap = minus, -minus
            put(2 * slot, total[0:64], total[64:128])
            put(2 * slot + 1, gap[64:128], -gap[0:64])

    width = 2048

    def sample(waves, add, first, last):
        rows = rows_of(waves)

        def one(index, _):
            where = pl.ds(pl.multiple_of(index * width, width), width)
            mixed = jnp.dot(
                sampler[0 : len(rows) * 64, :], pair_ref[:, where], preferred_element_type=f32
            )
            total = out_ref[:, where] if add else 0.0
            for slot, row in enumerate(rows):
                total = total + mixed[slot * 64 : (slot + 1) * 64] * lead_ref[row : row + 1, where]
            out_ref[:, where] = total
            return 0

        lax.fori_loop(first, last, one, 0)

    steps = atoms // chunk
    spread(cot_ref, ODD, 0, 0, steps)
    finish(0, ODD, 0)
    pl.semaphore_wait(barrier, CHIPS)
    mate_copy(0, 1).start()
    spread(cot_ref, EVEN, 8, 0, steps)
    finish(0, EVEN, 8)
    mate_copy(0, 0).start()
    to_owners(0, 1)
    load_feat.wait()
    every_wave = ODD + EVEN
    spread(feat_ref, every_wave, 0, 0, 1)
    to_owners(0, 0)
    spread(feat_ref, every_wave, 0, 1, 2)
    lay_weights()
    spread(feat_ref, every_wave, 0, 2, 3)

    @pl.when(parity == 1)
    def _():
        mix_and_share()

    spread(feat_ref, every_wave, 0, 3, steps)

    @pl.when(parity == 0)
    def _():
        mix_and_share()

    finish(1, every_wave, 0)
    mate_copy(1, 1).start()
    mate_copy(1, 0).start()
    forward(1)
    to_owners(1, 1)
    to_owners(1, 0)
    both_copy(1).wait_recv()
    build_sampler(1, ODD)
    half = atoms // width // 2
    sample(ODD, False, 0, half)
    forward(0)
    sample(ODD, False, half, 2 * half)
    both_copy(0).wait_recv()
    build_sampler(0, EVEN)
    sample(EVEN, True, 0, 2 * half)
    own_sum(1)
    for kind in range(2):
        for side in range(2):
            mate_copy(kind, side).wait_send()
        every = from_chip.at[kind]
        pltpu.make_async_copy(every, every, chip_send.at[kind]).wait()
    every = from_chip.at[0]
    pltpu.make_async_copy(every, every, grad_send).wait()
    both_copy(0).wait_send()
    both_copy(1).wait_send()


def fused_call(features, cotangent, positions, tiles, weight, scale):
    atoms = features.shape[1]
    vmem = pl.BlockSpec(memory_space=pltpu.VMEM)
    anywhere = pl.BlockSpec(memory_space=pl.ANY)
    return pl.pallas_call(
        functools.partial(fused_kernel, scale),
        out_shape=[
            jax.ShapeDtypeStruct((CHANNELS, atoms), f32),
            jax.ShapeDtypeStruct((2, MODES, 128), f32),
        ],
        in_specs=[pl.BlockSpec(memory_space=pltpu.SMEM), vmem, vmem, anywhere, anywhere],
        out_specs=[vmem, vmem],
        scratch_shapes=[
            pltpu.VMEM((CHANNELS, atoms), bf16),
            pltpu.VMEM(weight.shape, f32),
            pltpu.VMEM((2, CHANNELS // 2, MODES, 128), f32),
            pltpu.VMEM((2 * PAIRS, atoms), bf16),
            pltpu.VMEM((ROWS_L_PAD, atoms), f32),
            pltpu.VMEM((ROWS_L * CHANNELS, 2048), bf16),
            pltpu.VMEM((2 * PAIRS, (ROWS_L + 1) * CHANNELS), f32),
            pltpu.VMEM((2, 4, 2, 2, PAIRS, 128), bf16),
            pltpu.VMEM((2, 2, 4, PAIRS, 128), bf16),
            pltpu.VMEM((2, 2, 4, PAIRS, 128), bf16),
            pltpu.VMEM((2, CHIPS - 1, MODES, 128), bf16),
            pltpu.VMEM((4 * TILE_ROWS, 128), bf16),
            pltpu.VMEM((MODES, 128), bf16),
            pltpu.VMEM((2, 4, 2, PAIRS, 128), bf16),
            pltpu.VMEM((9 * CHANNELS, 2 * PAIRS), bf16),
            pltpu.SemaphoreType.DMA((2,)),
            pltpu.SemaphoreType.DMA((2, 2)),
            pltpu.SemaphoreType.DMA((2, 2)),
            pltpu.SemaphoreType.DMA((2,)),
            pltpu.SemaphoreType.DMA((2,)),
            pltpu.SemaphoreType.DMA,
            pltpu.SemaphoreType.DMA((2,)),
            pltpu.SemaphoreType.DMA((2,)),
            pltpu.SemaphoreType.DMA((2,)),
        ],
        compiler_params=pltpu.CompilerParams(
            collective_id=0, has_side_effects=True, vmem_limit_bytes=VMEM_LIMIT
        ),
        name="fused",
    )(tiles, positions, cotangent, features, weight)


def last_kernel(spectrum_ref, part_ref, out_ref, weight_hbm, columns, weight_out, store_sem):
    step = pl.program_id(0)
    store = pltpu.make_async_copy(weight_out, weight_hbm, store_sem)

    @pl.when(step == 0)
    def _():
        weight_gradient(spectrum_ref, weight_out, columns)
        store.start()

    out_ref[...] = part_ref[...]

    @pl.when(step == pl.num_programs(0) - 1)
    def _():
        store.wait()


def weight_gradient(spectrum_ref, out_ref, columns):
    lanes = lax.broadcasted_iota(jnp.int32, (MODES, 128), 1)
    spread_pair = jnp.where(
        lax.broadcasted_iota(jnp.int32, (128, 128), 0) % 2
        == lax.broadcasted_iota(jnp.int32, (128, 128), 1) // 64,
        1.0,
        0.0,
    ).astype(bf16)
    g_real, g_imag = both_halves(spectrum_ref[0], False), both_halves(spectrum_ref[0], True)
    real, imag = both_halves(spectrum_ref[1], False), both_halves(spectrum_ref[1], True)
    for tile in range(CHANNELS // 2):
        keep = lanes // 2 == tile
        columns[0, tile * MODES : (tile + 1) * MODES] = jnp.where(keep, real, 0.0)
        columns[1, tile * MODES : (tile + 1) * MODES] = jnp.where(keep, imag, 0.0)
    f_real = split_product(columns[0], spread_pair)
    f_imag = split_product(columns[1], spread_pair)
    for tile in range(CHANNELS // 2):
        rows = slice(tile * MODES, (tile + 1) * MODES)
        where = slice(tile * 128, (tile + 1) * 128)
        out_ref[:, 0, where] = f_real[rows] * g_real + f_imag[rows] * g_imag
        out_ref[:, 1, where] = f_real[rows] * g_imag - f_imag[rows] * g_real


def last_call(part, spectrum):
    atoms = part.shape[1]
    width = 2048
    weight_shape = (MODES, 2, CHANNELS * CHANNELS)
    return pl.pallas_call(
        last_kernel,
        grid=(atoms // width,),
        out_shape=[
            jax.ShapeDtypeStruct((CHANNELS, atoms), f32),
            jax.ShapeDtypeStruct(weight_shape, f32),
        ],
        in_specs=[
            pl.BlockSpec((2, MODES, 128), lambda i: (0, 0, 0)),
            pl.BlockSpec((CHANNELS, width), lambda i: (0, i)),
        ],
        out_specs=[
            pl.BlockSpec((CHANNELS, width), lambda i: (0, i)),
            pl.BlockSpec(memory_space=pl.ANY),
        ],
        scratch_shapes=[
            pltpu.VMEM((2, CHANNELS // 2 * MODES, 128), f32),
            pltpu.VMEM(weight_shape, f32),
            pltpu.SemaphoreType.DMA,
        ],
        compiler_params=pltpu.CompilerParams(vmem_limit_bytes=VMEM_LIMIT),
        name="last",
    )(spectrum, part)


def on_device(features, cotangent, positions, tiles, weight):
    devices_all = lax.axis_size("slab") * lax.axis_size("pencil")
    scale = 1.0 / math.sqrt(TILES_DEV * TILE * devices_all)
    gradient, spectrum = fused_call(features, cotangent, positions, tiles, weight, scale)
    return tuple(last_call(gradient, spectrum))


def solution(mesh):
    return jax.shard_map(
        on_device,
        mesh=mesh,
        in_specs=(
            P(None, ("slab", "pencil")),
            P(None, ("slab", "pencil")),
            P(None, ("slab", "pencil")),
            P(("slab", "pencil")),
            P(("slab", "pencil"), None, None),
        ),
        out_specs=(P(None, ("slab", "pencil")), P(("slab", "pencil"), None, None)),
        check_vma=False,
    )
```
